512 devices in a mesh: row: 16 (over x, y_hi, core), col: 32 (over z, y_lo).
Axes of the slice: x: 4, y: 8 (y_hi: 2, y_lo: 4; y = y_hi * 4 + y_lo), z: 8, core: 2. Of those that a mesh axis runs over, the one named last changes fastest.
Arguments:
- he_tiles: bfloat16 [128, 512, 768], P('row', 'col'), may hold values from -6 to 6
- ihc_tiles: bfloat16 [128, 512, 768], P('row', 'col'), may hold values from -6 to 6
- he_mask: int32 [128, 512], P('row', 'col'), may hold values from 0 to 1, as said below
- ihc_mask: int32 [128, 512], P('row', 'col'), may hold values from 0 to 1, as said below
- offsets: int32 [16, 64, 2], P('row', 'col'), may hold values from -4 to 4, as said below
- w_query: bfloat16 [768, 384], replicated, may hold values from -0.21875 to 0.21875
- w_key: bfloat16 [768, 384], replicated, may hold values from -0.21875 to 0.21875
- w_value: bfloat16 [768, 384], replicated, may hold values from -0.21875 to 0.21875
- grad_out: bfloat16 [128, 512, 384], P('row', 'col'), may hold values from -24 to 24
Outputs:
- he_grad: bfloat16 [128, 512, 768], P('row', 'col')
- ihc_grad: bfloat16 [128, 512, 768], P('row', 'col')
- weight_grads: float32 [3, 768, 384], P(None, 'row', 'col')
The draws below stay inside these ranges and needn't reach their ends.
Inputs may be any that keep to these rules, and one draw needn't show every extreme that they name: `he_mask`: 1 marks a tissue tile; the share of tissue tiles differs between the 8 x 16 tile blocks of the devices. `ihc_mask`: 1 marks a tissue tile; the share of tissue tiles differs between the 8 x 16 tile blocks of the devices. `offsets`: entry 0 shifts rows, entry 1 shifts columns of the key window of every tile in the block.
All inputs are finite; a program needn't handle non-finite values.
Results may differ from the reference program's by a relative error of at most 0.015.
Values may be sent and summed in bfloat16 or wider, within the bound.
A program may use at most 64 MiB of HBM per device.

```python
import math
import jax
import jax.numpy as jnp
from jax import lax

D = 768
HEADS = 6
HD = 64
BR = 8
BC = 16
OB = 8
R = 4
WIN = 5
NR = 128
NC = 512


def tissue_layout(key):
    first_key, second_key = jax.random.split(key)
    density = jax.random.randint(first_key, (NR // BR, NC // BC), 1, 9)
    tile_draw = jax.random.randint(second_key, (NR, NC), 0, 8)
    spread = jnp.repeat(jnp.repeat(density, BR, axis=0), BC, axis=1)
    return (tile_draw < spread).astype(jnp.int32)


def draw_he_mask(key, part):
    key = jax.random.fold_in(key, 3)
    return tissue_layout(key)


def draw_ihc_mask(key, part):
    key = jax.random.fold_in(key, 5)
    return tissue_layout(key)


def draw_offsets(key, part):
    key = jax.random.fold_in(key, 11)
    shifts = jax.random.randint(key, (NR // OB, NC // OB, 2), -R, R + 1)
    shifts = shifts.at[0, 0, :].set(R)
    shifts = shifts.at[0, 1, :].set(-R)
    return shifts.astype(jnp.int32)


def level_of(own_key, dims, shards, least, high):
    def one(axis_at, parts):
        steps = jax.random.uniform(jax.random.fold_in(jax.random.fold_in(own_key, 6), axis_at), (parts,), jnp.float32, least / len(shards), high / len(shards))
        return jnp.repeat(jnp.exp(steps), dims[axis_at] // parts).reshape((-1,) + (1,) * (len(dims) - axis_at - 1))

    gain = one(*shards[0])
    for cut in shards[1:]:
        gain = gain * one(*cut)
    return gain


def scatter_about(key, dims, width, bound, pieces=(), kind=jnp.bfloat16):
    gain = level_of(key, dims, pieces, -0.22, 0.18) if pieces else 1.0
    drawn = jax.random.normal(key, dims, jnp.float32) * width * gain
    return jnp.minimum(jnp.maximum(drawn, -bound), bound).astype(kind)


def setup_inputs(seed: int = 0) -> dict:
    arg_keys = jax.random.split(jax.random.key(seed), 10)
    he_tiles = scatter_about(arg_keys[0], (NR, NC, D), 1.0, 6.0, ((0, 16), (1, 32)))
    ihc_tiles = scatter_about(arg_keys[1], (NR, NC, D), 1.0, 6.0, ((0, 16), (1, 32)))
    he_mask = draw_he_mask(jax.random.fold_in(arg_keys[9], 71), 0)
    ihc_mask = draw_ihc_mask(jax.random.fold_in(arg_keys[9], 71), 0)
    offsets = draw_offsets(jax.random.fold_in(arg_keys[9], 71), 0)
    w_query = scatter_about(arg_keys[5], (D, HEADS * HD), D ** -0.5, 0.21875)
    w_key = scatter_about(arg_keys[6], (D, HEADS * HD), D ** -0.5, 0.21875)
    w_value = scatter_about(arg_keys[7], (D, HEADS * HD), D ** -0.5, 0.21875)
    grad_out = scatter_about(arg_keys[8], (NR, NC, HEADS * HD), 4.0, 24.0, ((0, 16), (1, 32)))
    return dict(he_tiles=he_tiles, ihc_tiles=ihc_tiles, he_mask=he_mask, ihc_mask=ihc_mask, offsets=offsets, w_query=w_query, w_key=w_key, w_value=w_value, grad_out=grad_out)


def reference(he_tiles, ihc_tiles, he_mask, ihc_mask, offsets, w_query, w_key, w_value, grad_out):
    head_width = HEADS * HD
    margin = R + WIN // 2
    radius = WIN // 2
    scaling = 1.0 / math.sqrt(HD)
    score_shift = -math.log(WIN * WIN)
    flat_he = he_tiles.reshape(NR * NC, D)
    flat_ihc = ihc_tiles.reshape(NR * NC, D)
    query_proj = jnp.dot(flat_he, w_query, preferred_element_type=jnp.float32).astype(jnp.bfloat16)
    key_proj = jnp.dot(flat_ihc, w_key, preferred_element_type=jnp.float32).astype(jnp.bfloat16)
    value_proj = jnp.dot(flat_ihc, w_value, preferred_element_type=jnp.float32).astype(jnp.bfloat16)
    pad_spec = ((margin, margin), (margin, margin), (0, 0))
    key_pad = jnp.pad(key_proj.reshape(NR, NC, head_width), pad_spec)
    value_pad = jnp.pad(value_proj.reshape(NR, NC, head_width), pad_spec)
    mask_pad = jnp.pad(ihc_mask.astype(jnp.float32), margin)
    shift_rows = jnp.repeat(jnp.repeat(offsets[:, :, 0], OB, axis=0), OB, axis=1).astype(jnp.int32)
    shift_cols = jnp.repeat(jnp.repeat(offsets[:, :, 1], OB, axis=0), OB, axis=1).astype(jnp.int32)
    base_rows = lax.broadcasted_iota(jnp.int32, (NR, NC), 0) + shift_rows + margin - radius
    base_cols = lax.broadcasted_iota(jnp.int32, (NR, NC), 1) + shift_cols + margin - radius
    query32 = query_proj.astype(jnp.float32).reshape(NR, NC, HEADS, HD)
    grad32 = grad_out.astype(jnp.float32).reshape(NR, NC, HEADS, HD)
    query_open = he_mask.astype(jnp.float32)[:, :, None]
    query_acc = jnp.zeros((NR, NC, HEADS, HD), jnp.float32)
    canvas_key = jnp.zeros(key_pad.shape, jnp.float32)
    canvas_value = jnp.zeros(key_pad.shape, jnp.float32)
    for step_row in range(WIN):
        for step_col in range(WIN):
            row_index = (base_rows + step_row).astype(jnp.int32)
            col_index = (base_cols + step_col).astype(jnp.int32)
            key_seen = key_pad[row_index, col_index].astype(jnp.float32).reshape(NR, NC, HEADS, HD)
            value_seen = value_pad[row_index, col_index].astype(jnp.float32).reshape(NR, NC, HEADS, HD)
            key_open = mask_pad[row_index, col_index][:, :, None]
            scores = lax.optimization_barrier(jnp.sum(query32 * key_seen, axis=-1)) * scaling
            sigmoid_val = jax.nn.sigmoid(scores + score_shift)
            open_gate = query_open * key_open
            weight = open_gate * sigmoid_val
            dweight = lax.optimization_barrier(jnp.sum(grad32 * value_seen, axis=-1))
            dscore = dweight * open_gate * sigmoid_val * (1.0 - sigmoid_val) * scaling
            query_acc = query_acc + dscore[..., None] * key_seen
            canvas_key = canvas_key.at[row_index, col_index].add((dscore[..., None] * query32).reshape(NR, NC, head_width))
            canvas_value = canvas_value.at[row_index, col_index].add((weight[..., None] * grad32).reshape(NR, NC, head_width))
    query_grad = query_acc.reshape(NR * NC, head_width).astype(jnp.bfloat16)
    key_grad = canvas_key[margin:margin + NR, margin:margin + NC].reshape(NR * NC, head_width).astype(jnp.bfloat16)
    value_grad = canvas_value[margin:margin + NR, margin:margin + NC].reshape(NR * NC, head_width).astype(jnp.bfloat16)
    back_dims = (((1,), (1,)), ((), ()))
    he_grad = lax.dot_general(query_grad, w_query, back_dims, preferred_element_type=jnp.float32)
    he_grad = he_grad.astype(jnp.bfloat16).reshape(NR, NC, D)
    ihc_sum = lax.dot_general(key_grad, w_key, back_dims, preferred_element_type=jnp.float32)
    ihc_sum = ihc_sum + lax.dot_general(value_grad, w_value, back_dims, preferred_element_type=jnp.float32)
    ihc_grad = ihc_sum.astype(jnp.bfloat16).reshape(NR, NC, D)
    tile_dims = (((0,), (0,)), ((), ()))
    grad_query_w = lax.dot_general(flat_he, query_grad, tile_dims, preferred_element_type=jnp.float32)
    grad_key_w = lax.dot_general(flat_ihc, key_grad, tile_dims, preferred_element_type=jnp.float32)
    grad_value_w = lax.dot_general(flat_ihc, value_grad, tile_dims, preferred_element_type=jnp.float32)
    norm_scale = 1.0 / math.sqrt(NR * NC)
    weight_grads = jnp.stack([grad_query_w, grad_key_w, grad_value_w]) * norm_scale
    return (he_grad, ihc_grad, weight_grads)
```

```python
import functools
import math

import jax
import jax.numpy as jnp
import numpy as np
from jax import lax
from jax.experimental import pallas as pl
from jax.experimental.pallas import tpu as pltpu
from jax.sharding import PartitionSpec as P

MESH = pl.DeviceIdType.MESH
BF = jnp.bfloat16
F32 = jnp.float32
PAIRS = 3
OWN, NEAR, SIDE, NSIDE, FAR, CORNER, ROWS = 0, 128, 224, 320, 416, 512, 608
QL = 896
S_NEAR, S_FAR, S_RIGHT, S_LEFT, S_FWD, S_CR, S_CL = 0, 2, 4, 6, 8, 10, 12
S_HX, S_DKV, S_DQ, S_X, S_Y, S_Z, S_ALL = 14, 15, 16, 17, 23, 30, 37


def constants():
    n = np.arange(48)
    pack = np.zeros((96, 128), np.float32)
    pack[n, (n // 6) * 16 + 10 + n % 6] = 1
    pack[48 + n, (n // 6) * 16 + n % 6] = 1
    corner = np.zeros((96, 96), np.float32)
    m = np.arange(36)
    corner[m, (m // 6) * 16 + 10 + m % 6] = 1
    corner[48 + m, (m // 6) * 16 + m % 6] = 1
    perm = np.zeros((768, 768), np.float32)
    f = np.arange(768)
    slab, inner = f // 48, f % 48
    perm[f, (slab % 2) * 384 + (slab // 2) * 48 + inner] = 1
    to_y = np.zeros((384, 512), np.float32)
    lane = np.arange(384)
    c, j = lane // 12, lane % 12
    to_y[lane, (c % 4) * 128 + (c // 4) * 12 + j] = 1
    to_z = np.zeros((384, 1024), np.float32)
    for part in range(3):
        k = np.arange(96)
        to_z[part * 128 + k, (k // 12) * 128 + part * 12 + k % 12] = 1
    spread = np.zeros((128, 256), np.float32)
    spread[0, :128] = 1
    spread[64, 128:] = 1
    place = np.zeros((2, ROWS, 128), np.float32)
    for core in range(2):
        near0, far0 = (8, -6) if core == 0 else (-6, 8)
        own = np.arange(128)
        row, col = np.zeros(ROWS), np.zeros(ROWS)
        row[:128], col[:128] = own // 16, own % 16
        w = np.arange(96)
        row[NEAR : NEAR + 96], col[NEAR : NEAR + 96] = near0 + w // 16, w % 16
        row[FAR : FAR + 96], col[FAR : FAR + 96] = far0 + w // 16, w % 16
        s = w % 48
        scol = np.where(w < 48, -6 + s % 6, 16 + s % 6)
        row[SIDE : SIDE + 96], col[SIDE : SIDE + 96] = s // 6, scol
        row[NSIDE : NSIDE + 96] = (8 if core == 0 else -8) + s // 6
        col[NSIDE : NSIDE + 96] = scol
        row[CORNER : CORNER + 96], col[CORNER : CORNER + 96] = far0 + s // 6, scol
        place[core, :, 0] = row
        place[core, :, 64] = col
    return [jnp.asarray(a, BF) for a in (pack, corner, perm, to_y, to_z, spread, place)]


def dot(a, b, dims=((1,), (0,))):
    return lax.dot_general(a, b, (dims, ((), ())), preferred_element_type=F32)


def kernel(
    rows, cols,
    off_ref, he_ref, ihc_ref, hm_ref, im_ref, wq_ref, wk_ref, wv_ref, g_ref,
    pack_ref, corner_ref, perm_ref, toy_ref, toz_ref, spread_ref, place_ref,
    heg_ref, ihcg_ref, wg_ref,
    qg, kv, pq, pk, cq, ck, place, bd, acc, hp, hx, dmine, dother, dw,
    xs_q, xr_q, xs_kv, xr_kv, ys, yr, zs, zr, send_sem, recv_sem,
):
    r, c = lax.axis_index("row"), lax.axis_index("col")
    x, yh, core = r // 4, lax.rem(r // 2, 2), lax.rem(r, 2)
    z, yl = c // 4, lax.rem(c, 4)
    y = yh * 4 + yl
    nx, nz = rows // 4, cols // 4
    near = (r + 1 - 2 * core, c)
    far = (lax.rem(r + 2 * core - 1 + rows, rows), c)
    right = (r, lax.rem(c + 1, cols))
    left = (r, lax.rem(c + cols - 1, cols))
    x_peers = [(lax.rem(x + d, nx), d) for d in range(1, nx)]
    y_peers = [(lax.rem(y + d, 8), d) for d in range(1, 8)]
    z_peers = [(lax.rem(z + d, nz), d) for d in range(1, nz)]

    def x_dev(v):
        return (v * 4 + yh * 2 + core, c)

    def y_dev(v):
        return (x * 4 + (v // 4) * 2 + core, z * 4 + lax.rem(v, 4))

    def z_dev(v):
        return (r, v * 4 + yl)

    partners = [near, far, right, left]
    partners += [x_dev(v) for v, _ in x_peers]
    partners += [y_dev(v) for v, _ in y_peers]
    partners += [z_dev(v) for v, _ in z_peers]
    barrier = pltpu.get_barrier_semaphore()
    for dev in partners:
        pl.semaphore_signal(barrier, inc=1, device_id=dev, device_id_type=MESH)

    started = []

    def send(src, dst, sem, dev):
        cp = pltpu.make_async_remote_copy(
            src_ref=src, dst_ref=dst, send_sem=send_sem.at[sem], recv_sem=recv_sem.at[sem],
            device_id=dev, device_id_type=MESH,
        )
        cp.start()
        started.append(cp)
        return cp

    q = dot(he_ref[...], wq_ref[...]).astype(BF)
    qg[0:128, 0:384] = q
    qg[0:128, 384:768] = (g_ref[...].astype(F32) * hm_ref[...]).astype(BF)
    tile = lax.broadcasted_iota(jnp.int32, (128, 128), 0)
    lane = lax.broadcasted_iota(jnp.int32, (128, 128), 1)
    a0, b0 = off_ref[0].astype(F32), off_ref[1].astype(F32)
    a1, b1 = off_ref[2].astype(F32), off_ref[3].astype(F32)
    first = lax.rem(tile, 16) < 8
    qg[0:128, 768:896] = jnp.where(
        lane < 64, jnp.where(first, a0, a1), jnp.where(first, b0, b1)
    ).astype(BF)
    pq[...] = dot(pack_ref[...], qg[0:128, :]).astype(BF)
    ihc = ihc_ref[...]
    kv[0:128, 0:384] = (dot(ihc, wk_ref[...]) * im_ref[...]).astype(BF)
    kv[0:128, 384:768] = (dot(ihc, wv_ref[...]) * im_ref[...]).astype(BF)
    pk[...] = dot(pack_ref[...], kv[0:128, :]).astype(BF)

    pl.semaphore_wait(barrier, len(partners))

    near_at = pl.ds(pl.multiple_of(32 * (1 - core), 32), 96)
    far_at = pl.ds(pl.multiple_of(32 * core, 32), 96)

    def rng(start, size=96):
        return pl.ds(start, size)

    cps = {}
    for t, (buf, packed) in enumerate(((qg, pq), (kv, pk))):
        cps["far", t] = send(buf.at[far_at], buf.at[rng(FAR)], S_FAR + t, far)
        cps["right", t] = send(packed.at[rng(0, 48)], buf.at[rng(SIDE, 48)], S_RIGHT + t, right)
        cps["left", t] = send(
            packed.at[rng(48, 48)], buf.at[rng(SIDE + 48, 48)], S_LEFT + t, left
        )
        cps["near", t] = send(buf.at[near_at], buf.at[rng(NEAR)], S_NEAR + t, near)

    for t, ref in enumerate((he_ref, ihc_ref)):
        ordered = dot(ref[...], perm_ref[...]).astype(BF)
        hp[0, t] = ordered[:, 0:384]
        hp[1, t] = ordered[:, 384:768]
    cps["hx"] = send(hp.at[1 - core], hx, S_HX, near)

    place[...] = place_ref[core]
    row_bad = jnp.where(core == 0, (r == 0).astype(F32), (r == rows - 1).astype(F32)) * 1024.0
    left_bad = (c == 0).astype(F32) * 1024.0
    right_bad = (c == cols - 1).astype(F32) * 1024.0

    def shift(start, size, amount):
        place[start : start + size, :] = (
            place[start : start + size, :].astype(F32) + amount
        ).astype(BF)

    for base in (SIDE, NSIDE):
        shift(base, 48, left_bad)
        shift(base + 48, 48, right_bad)
    shift(FAR, 96, row_bad)
    shift(CORNER, 48, left_bad + row_bad)
    shift(CORNER + 48, 48, right_bad + row_bad)

    low = lane < 64
    zero = jnp.zeros((128, 128), BF)
    for i, (buf, base) in enumerate(((kv, 0), (kv, 384), (qg, 0), (qg, 384))):
        for h in range(PAIRS):
            part = buf[0:128, base + 128 * h : base + 128 * h + 128]
            bd[i, h, 0:128, :] = jnp.where(low, part, zero)
            bd[i, h, 128:256, :] = jnp.where(low, zero, part)
    acc[...] = jnp.zeros(acc.shape, F32)

    vec = lax.broadcasted_iota(jnp.int32, (1, 128), 1)
    lane_row = (vec // 16).astype(F32)
    lane_col = lax.rem(vec, 16).astype(F32)
    vfirst = lax.rem(vec, 16) < 8
    aim_row = lane_row + jnp.where(vfirst, a0, a1)
    aim_col = lane_col + jnp.where(vfirst, b0, b1)
    shift_open = math.log(25.0)

    def attend(part, start, size):
        buf = (qg, kv)[part]
        where_at = place[start : start + size, :]
        if part == 0:
            where_at = where_at + qg[start : start + size, 768:896]
        at = dot(where_at, spread_ref[...])
        lr, lc = (lane_row, lane_col) if part == 0 else (aim_row, aim_col)
        gap = jnp.maximum(jnp.abs(at[:, 0:128] - lr), jnp.abs(at[:, 128:256] - lc))
        bias = jnp.where(gap <= 2.5, shift_open, 1e9)
        bias = jnp.concatenate([bias, bias], axis=1)
        for h in range(PAIRS):
            one = buf[start : start + size, 128 * h : 128 * h + 128]
            two = buf[start : start + size, 384 + 128 * h : 384 + 128 * h + 128]
            score = dot(one, bd[2 * part, h], ((1,), (1,)))
            dweight = dot(two, bd[2 * part + 1, h], ((1,), (1,)))
            e = jnp.exp(jnp.minimum(bias - score * 0.125, 88.0))
            sig = 1.0 / (1.0 + e)
            dscore = (dweight * (sig * (1.0 - sig))).astype(BF)
            acc[part, h] += dot(dscore, one, ((0,), (0,)))
            if part == 0:
                acc[2, h] += dot(sig.astype(BF), two, ((0,), (0,)))

    def gather(i, scale):
        parts = [jnp.where(low, acc[i, h, 0:128], acc[i, h, 128:256]) * scale for h in range(PAIRS)]
        return jnp.concatenate(parts, axis=1)

    attend(0, OWN, 128)
    attend(1, OWN, 128)
    for t in range(2):
        cps["near", t].wait_recv()
        attend(t, NEAR, 96)
    for t, buf in enumerate((qg, kv)):
        cps["right", t].wait_recv()
        cps["left", t].wait_recv()
        cps["fwd", t] = send(buf.at[rng(SIDE)], buf.at[rng(NSIDE)], S_FWD + t, near)
        attend(t, SIDE, 96)

    def corners(t, buf, packed):
        cps["far", t].wait_recv()
        packed[...] = dot(corner_ref[...], buf[FAR : FAR + 96, :]).astype(BF)
        cps["cr", t] = send(packed.at[rng(0, 48)], buf.at[rng(CORNER, 48)], S_CR + t, right)
        cps["cl", t] = send(packed.at[rng(48, 48)], buf.at[rng(CORNER + 48, 48)], S_CL + t, left)

    corners(0, qg, cq)
    for t in range(2):
        cps["fwd", t].wait_recv()
        attend(t, NSIDE, 96)
    attend(0, FAR, 96)
    corners(1, kv, ck)
    cps["cr", 0].wait_recv()
    cps["cl", 0].wait_recv()
    attend(0, CORNER, 96)

    dk = gather(0, 0.125).astype(BF)
    dv = (gather(2, 1.0) * im_ref[...]).astype(BF)
    dmine[1] = dk
    dmine[2] = dv
    cps["dkv"] = send(dmine.at[pl.ds(1, 2)], dother.at[pl.ds(1, 2)], S_DKV, near)
    attend(1, FAR, 96)
    cps["hx"].wait_recv()
    cps["dkv"].wait_recv()

    def partial(m, t):
        total = dot(hp[core, t], dmine[m], ((0,), (0,)))
        return total + dot(hx[t], dother[m], ((0,), (0,)))

    for m in (1, 2):
        w = partial(m, 1)
        for i in range(nx):
            piece = w[96 * i : 96 * i + 96]
            dw[i, :, 384 * m : 384 * m + 384] = piece
            xs_kv[i, :, 384 * (m - 1) : 384 * m] = piece.astype(BF)
    for v, d in x_peers:
        cps["xkv", d] = send(xs_kv.at[v], xr_kv.at[d - 1], S_X + d - 1, x_dev(v))
    cps["cr", 1].wait_recv()
    cps["cl", 1].wait_recv()
    attend(1, CORNER, 96)
    dq = gather(1, 0.125).astype(BF)
    dmine[0] = dq
    cps["dq"] = send(dmine.at[0], dother.at[0], S_DQ, near)
    heg_ref[...] = dot(dq, wq_ref[...], ((1,), (1,))).astype(BF)
    cps["dq"].wait_recv()
    w = partial(0, 0)
    for i in range(nx):
        piece = w[96 * i : 96 * i + 96]
        dw[i, :, 0:384] = piece
        xs_q[i] = piece.astype(BF)
    for v, d in x_peers:
        cps["xq", d] = send(xs_q.at[v], xr_q.at[d - 1], S_X + 3 + d - 1, x_dev(v))
    ihcg_ref[...] = (
        dot(dk, wk_ref[...], ((1,), (1,))) + dot(dv, wv_ref[...], ((1,), (1,)))
    ).astype(BF)

    def to_y(m, total):
        laid = dot(total.astype(BF), toy_ref[...]).astype(BF)
        for h in range(2):
            for l in range(4):
                ys[4 * h + l, :, 128 * m : 128 * m + 128] = laid[
                    48 * h : 48 * h + 48, 128 * l : 128 * l + 128
                ]

    for _, d in x_peers:
        cps["xkv", d].wait_recv()
    for m in (1, 2):
        total = dw[x, :, 384 * m : 384 * m + 384]
        for _, d in x_peers:
            total = total + xr_kv[d - 1, :, 384 * (m - 1) : 384 * m].astype(F32)
        to_y(m, total)
    for _, d in x_peers:
        cps["xq", d].wait_recv()
    total = dw[x, :, 0:384]
    for _, d in x_peers:
        total = total + xr_q[d - 1].astype(F32)
    to_y(0, total)
    for v, d in y_peers:
        cps["y", d] = send(ys.at[v], yr.at[d - 1], S_Y + d - 1, y_dev(v))
    total = ys[y].astype(F32)
    for _, d in y_peers:
        cps["y", d].wait_recv()
        total = total + yr[d - 1].astype(F32)
    laid = dot(total.astype(BF), toz_ref[...]).astype(BF)
    for i in range(nz):
        zs[i] = laid[:, 128 * i : 128 * i + 128]
    for v, d in z_peers:
        cps["z", d] = send(zs.at[v], zr.at[d - 1], S_Z + d - 1, z_dev(v))
    total = zs[z].astype(F32)
    for _, d in z_peers:
        cps["z", d].wait_recv()
        total = total + zr[d - 1].astype(F32)
    total = total * (1.0 / math.sqrt(128.0 * rows * cols))
    for m in range(3):
        wg_ref[m] = total[:, 12 * m : 12 * m + 12]
    for cp in started:
        cp.wait_send()


def on_device(rows, cols, he, ihc, he_mask, ihc_mask, offsets, wq, wk, wv, grad_out):
    nx, nz = rows // 4, cols // 4
    vm = pl.BlockSpec(memory_space=pltpu.VMEM)
    consts = constants()
    args = (
        offsets.reshape(4),
        he.reshape(128, 768), ihc.reshape(128, 768),
        he_mask.reshape(128, 1).astype(F32), ihc_mask.reshape(128, 1).astype(F32),
        wq, wk, wv, grad_out.reshape(128, 384), *consts,
    )
    heg, ihcg, wg = pl.pallas_call(
        functools.partial(kernel, rows, cols),
        out_shape=(
            jax.ShapeDtypeStruct((128, 768), BF),
            jax.ShapeDtypeStruct((128, 768), BF),
            jax.ShapeDtypeStruct((3, 48, 12), F32),
        ),
        in_specs=[pl.BlockSpec(memory_space=pltpu.SMEM)] + [vm] * (len(args) - 1),
        out_specs=(vm, vm, vm),
        scratch_shapes=[
            pltpu.VMEM((ROWS, QL), BF),
            pltpu.VMEM((ROWS, 768), BF),
            pltpu.VMEM((96, QL), BF),
            pltpu.VMEM((96, 768), BF),
            pltpu.VMEM((96, QL), BF),
            pltpu.VMEM((96, 768), BF),
            pltpu.VMEM((ROWS, 128), BF),
            pltpu.VMEM((4, PAIRS, 256, 128), BF),
            pltpu.VMEM((3, PAIRS, 256, 128), F32),
            pltpu.VMEM((2, 2, 128, 384), BF),
            pltpu.VMEM((2, 128, 384), BF),
            pltpu.VMEM((3, 128, 384), BF),
            pltpu.VMEM((3, 128, 384), BF),
            pltpu.VMEM((nx, 96, 1152), F32),
            pltpu.VMEM((nx, 96, 384), BF),
            pltpu.VMEM((nx - 1, 96, 384), BF),
            pltpu.VMEM((nx, 96, 768), BF),
            pltpu.VMEM((nx - 1, 96, 768), BF),
            pltpu.VMEM((8, 48, 384), BF),
            pltpu.VMEM((7, 48, 384), BF),
            pltpu.VMEM((nz, 48, 128), BF),
            pltpu.VMEM((nz - 1, 48, 128), BF),
            pltpu.SemaphoreType.DMA((S_ALL,)),
            pltpu.SemaphoreType.DMA((S_ALL,)),
        ],
        compiler_params=pltpu.CompilerParams(
            collective_id=0, has_side_effects=True, vmem_limit_bytes=40 << 20
        ),
    )(*args)
    return heg.reshape(8, 16, 768), ihcg.reshape(8, 16, 768), wg


def solution(mesh):
    placed = (
        P("row", "col", None), P("row", "col", None), P("row", "col"), P("row", "col"),
        P("row", "col", None), P(), P(), P(), P("row", "col", None),
    )
    return jax.shard_map(
        functools.partial(on_device, mesh.shape["row"], mesh.shape["col"]),
        mesh=mesh,
        in_specs=placed,
        out_specs=(P("row", "col", None), P("row", "col", None), P(None, "row", "col")),
        check_vma=False,
    )
```

```python
import functools
import math

import jax
import jax.numpy as jnp
import numpy as np
from jax import lax
from jax.experimental import pallas as pl
from jax.experimental.pallas import tpu as pltpu
from jax.sharding import PartitionSpec as P

MESH = pl.DeviceIdType.MESH
BF = jnp.bfloat16
F32 = jnp.float32
PAIRS = 3
OWN, NEAR, SIDE, NSIDE, FAR, CORNER, ROWS = 0, 128, 224, 320, 416, 512, 608
S_NEAR, S_FAR, S_RIGHT, S_LEFT, S_FWD, S_CR, S_CL = 0, 3, 6, 9, 12, 15, 18
S_HX, S_DKV, S_DQ, S_X, S_YKV, S_YQ, S_Z, S_ALL = 21, 22, 23, 24, 30, 37, 44, 51
I_OWN, I_NEAR, I_SIDE, I_NSIDE, I_FAR, I_CORNER, I_ALL = 0, 1, 2, 4, 6, 7, 9


def constants():
    n = np.arange(48)
    pack = np.zeros((96, 128), np.float32)
    pack[n, (n // 6) * 16 + 10 + n % 6] = 1
    pack[48 + n, (n // 6) * 16 + n % 6] = 1
    perm = np.zeros((768, 768), np.float32)
    f = np.arange(768)
    slab, inner = f // 48, f % 48
    perm[f, (slab % 2) * 384 + (slab // 2) * 48 + inner] = 1
    to_y = np.zeros((384, 512), np.float32)
    lane = np.arange(384)
    c, j = lane // 12, lane % 12
    to_y[lane, (c % 4) * 128 + (c // 4) * 12 + j] = 1
    to_z = np.zeros((384, 1024), np.float32)
    for part in range(3):
        k = np.arange(96)
        to_z[part * 128 + k, (k // 12) * 128 + part * 12 + k % 12] = 1
    spread = np.zeros((128, 256), np.float32)
    spread[0, :128] = 1
    spread[64, 128:] = 1
    place = np.zeros((2, ROWS, 128), np.float32)
    for core in range(2):
        near0, far0 = (8, -6) if core == 0 else (-6, 8)
        own = np.arange(128)
        row, col = np.zeros(ROWS), np.zeros(ROWS)
        row[:128], col[:128] = own // 16, own % 16
        w = np.arange(96)
        row[NEAR : NEAR + 96], col[NEAR : NEAR + 96] = near0 + w // 16, w % 16
        row[FAR : FAR + 96], col[FAR : FAR + 96] = far0 + w // 16, w % 16
        s = w % 48
        scol = np.where(w < 48, -6 + s % 6, 16 + s % 6)
        row[SIDE : SIDE + 96], col[SIDE : SIDE + 96] = s // 6, scol
        row[NSIDE : NSIDE + 96] = (8 if core == 0 else -8) + s // 6
        col[NSIDE : NSIDE + 96] = scol
        row[CORNER : CORNER + 96] = (-8 if core == 0 else 8) + s // 6
        col[CORNER : CORNER + 96] = scol
        place[core, :, 0] = row
        place[core, :, 64] = col
    return [jnp.asarray(a, BF) for a in (pack, perm, to_y, to_z, spread, place)]


def dot(a, b, dims=((1,), (0,))):
    return lax.dot_general(a, b, (dims, ((), ())), preferred_element_type=F32)


def kernel(
    rows, cols,
    off_in, he_in, ihc_in, hm_in, im_in, wq_in, wk_in, wv_in, g_in,
    pack_in, perm_in, toy_in, toz_in, spread_in, place_in,
    heg_ref, ihcg_ref, wg_ref,
    off_ref, he_ref, ihc_ref, hm_ref, im_ref, wq_ref, wk_ref, wv_ref, g_ref,
    pack_ref, perm_ref, toy_ref, toz_ref, spread_ref, place_ref, in_sem,
    qg, kv, pq, pk, info, place, bd, acc, hp, hx, dmine, dother, dw,
    xs_q, xr_q, xs_kv, xr_kv, ys_q, yr_q, ys_kv, yr_kv, zs, zr, send_sem, recv_sem,
):
    r, c = lax.axis_index("row"), lax.axis_index("col")
    x, yh, core = r // 4, lax.rem(r // 2, 2), lax.rem(r, 2)
    z, yl = c // 4, lax.rem(c, 4)
    y = yh * 4 + yl
    nx, nz = rows // 4, cols // 4
    near = (r + 1 - 2 * core, c)
    far = (lax.rem(r + 2 * core - 1 + rows, rows), c)
    right = (r, lax.rem(c + 1, cols))
    left = (r, lax.rem(c + cols - 1, cols))
    far_right, far_left = (far[0], right[1]), (far[0], left[1])
    x_peers = [(lax.rem(x + d, nx), d) for d in range(1, nx)]
    y_peers = [(lax.rem(y + d, 8), d) for d in range(1, 8)]
    z_peers = [(lax.rem(z + d, nz), d) for d in range(1, nz)]

    def x_dev(v):
        return (v * 4 + yh * 2 + core, c)

    def y_dev(v):
        return (x * 4 + (v // 4) * 2 + core, z * 4 + lax.rem(v, 4))

    def z_dev(v):
        return (r, v * 4 + yl)

    partners = [near, far, right, left, far_right, far_left]
    partners += [x_dev(v) for v, _ in x_peers]
    partners += [y_dev(v) for v, _ in y_peers]
    partners += [z_dev(v) for v, _ in z_peers]
    barrier = pltpu.get_barrier_semaphore()
    for dev in partners:
        pl.semaphore_signal(barrier, inc=1, device_id=dev, device_id_type=MESH)

    loads = {}
    order = (
        (he_in, he_ref), (wq_in, wq_ref), (g_in, g_ref), (hm_in, hm_ref), (off_in, off_ref),
        (pack_in, pack_ref), (ihc_in, ihc_ref), (wk_in, wk_ref), (wv_in, wv_ref),
        (im_in, im_ref), (perm_in, perm_ref), (place_in, place_ref), (spread_in, spread_ref),
        (toy_in, toy_ref), (toz_in, toz_ref),
    )
    for i, (src, dst) in enumerate(order):
        loads[i] = pltpu.make_async_copy(src, dst, in_sem.at[i])
        loads[i].start()

    def ready(*which):
        for i in which:
            loads[i].wait()

    started = []

    def send(src, dst, sem, dev):
        cp = pltpu.make_async_remote_copy(
            src_ref=src, dst_ref=dst, send_sem=send_sem.at[sem], recv_sem=recv_sem.at[sem],
            device_id=dev, device_id_type=MESH,
        )
        cp.start()
        started.append(cp)
        return cp

    tile = lax.broadcasted_iota(jnp.int32, (128, 128), 0)
    lane = lax.broadcasted_iota(jnp.int32, (128, 128), 1)

    def column(mask):
        mine = (tile[:, 0:8] // 16 == lane[:, 0:8]).astype(F32)
        spread = dot(mine, mask.astype(F32))
        here = lax.rem(tile[:, 0:16], 16) == lane[:, 0:16]
        return jnp.sum(jnp.where(here, spread, 0.0), axis=1, keepdims=True)

    ready(0, 1)
    q = dot(he_ref[...], wq_ref[...]).astype(BF)
    qg[0:128, 0:384] = q
    ready(2, 3, 4, 5)
    qg[0:128, 384:768] = (g_ref[...].astype(F32) * column(hm_ref[...])).astype(BF)
    off = off_ref[0].astype(F32)
    a0, b0, a1, b1 = off[0:1, 0:1], off[0:1, 1:2], off[1:2, 0:1], off[1:2, 1:2]
    block = jnp.where(lane < 64, jnp.where(tile == 0, a0, a1), jnp.where(tile == 0, b0, b1))
    info[I_OWN] = block[0:16].astype(BF)
    pq[...] = dot(pack_ref[...], qg[0:128, :]).astype(BF)
    ready(6, 7, 8, 9)
    ihc = ihc_ref[...]
    key_open = column(im_ref[...])
    kv[0:128, 0:384] = (dot(ihc, wk_ref[...]) * key_open).astype(BF)
    kv[0:128, 384:768] = (dot(ihc, wv_ref[...]) * key_open).astype(BF)
    pk[...] = dot(pack_ref[...], kv[0:128, :]).astype(BF)

    pl.semaphore_wait(barrier, len(partners))

    near_at = pl.ds(pl.multiple_of(32 * (1 - core), 32), 96)
    far_at = pl.ds(pl.multiple_of(32 * core, 32), 96)

    def rng(start, size=96):
        return pl.ds(start, size)

    cps = {}
    own_info = info.at[I_OWN]
    cps["far", 2] = send(own_info, info.at[I_FAR], S_FAR + 2, far)
    cps["near", 2] = send(own_info, info.at[I_NEAR], S_NEAR + 2, near)
    cps["right", 2] = send(own_info, info.at[I_SIDE], S_RIGHT + 2, right)
    cps["left", 2] = send(own_info, info.at[I_SIDE + 1], S_LEFT + 2, left)
    cps["cr", 2] = send(own_info, info.at[I_CORNER], S_CR + 2, far_right)
    cps["cl", 2] = send(own_info, info.at[I_CORNER + 1], S_CL + 2, far_left)
    for t, (buf, packed) in enumerate(((qg, pq), (kv, pk))):
        to_right, to_left = packed.at[rng(0, 48)], packed.at[rng(48, 48)]
        cps["far", t] = send(buf.at[far_at], buf.at[rng(FAR)], S_FAR + t, far)
        cps["right", t] = send(to_right, buf.at[rng(SIDE, 48)], S_RIGHT + t, right)
        cps["left", t] = send(to_left, buf.at[rng(SIDE + 48, 48)], S_LEFT + t, left)
        cps["cr", t] = send(to_right, buf.at[rng(CORNER, 48)], S_CR + t, far_right)
        cps["cl", t] = send(to_left, buf.at[rng(CORNER + 48, 48)], S_CL + t, far_left)
        cps["near", t] = send(buf.at[near_at], buf.at[rng(NEAR)], S_NEAR + t, near)

    ready(*range(10, 15))
    for t, ref in enumerate((he_ref, ihc_ref)):
        ordered = dot(ref[...], perm_ref[...]).astype(BF)
        hp[0, t] = ordered[:, 0:384]
        hp[1, t] = ordered[:, 384:768]
    cps["hx"] = send(hp.at[1 - core], hx, S_HX, near)

    place[...] = place_ref[core]
    row_bad = jnp.where(core == 0, (r == 0).astype(F32), (r == rows - 1).astype(F32)) * 1024.0
    left_bad = (c == 0).astype(F32) * 1024.0
    right_bad = (c == cols - 1).astype(F32) * 1024.0

    def shift(start, size, amount):
        place[start : start + size, :] = (
            place[start : start + size, :].astype(F32) + amount
        ).astype(BF)

    for base in (SIDE, NSIDE):
        shift(base, 48, left_bad)
        shift(base + 48, 48, right_bad)
    shift(FAR, 96, row_bad)
    shift(CORNER, 48, left_bad + row_bad)
    shift(CORNER + 48, 48, right_bad + row_bad)

    low = lane < 64
    zero = jnp.zeros((128, 128), BF)
    for i, (buf, base) in enumerate(((kv, 0), (kv, 384), (qg, 0), (qg, 384))):
        for h in range(PAIRS):
            part = buf[0:128, base + 128 * h : base + 128 * h + 128]
            bd[i, h, 0:128, :] = jnp.where(low, part, zero)
            bd[i, h, 128:256, :] = jnp.where(low, zero, part)
    acc[...] = jnp.zeros(acc.shape, F32)

    vec = lax.broadcasted_iota(jnp.int32, (1, 128), 1)
    lane_row = (vec // 16).astype(F32)
    lane_col = lax.rem(vec, 16).astype(F32)
    vfirst = lax.rem(vec, 16) < 8
    aim_row = lane_row + jnp.where(vfirst, a0, a1)
    aim_col = lane_col + jnp.where(vfirst, b0, b1)
    shift_open = math.log(25.0)

    slots = {NEAR: I_NEAR, SIDE: I_SIDE, NSIDE: I_NSIDE, FAR: I_FAR, CORNER: I_CORNER}

    def shifts(start, size):
        slot = slots.get(start, I_OWN)
        if start in (SIDE, NSIDE, CORNER):
            chosen = jnp.where(tile[0:size, 0:32] < 48, 1, 16) == lane[0:size, 0:32]
            table = jnp.concatenate([info[slot], info[slot + 1]], axis=0)
        else:
            chosen = lax.rem(tile[0:size, 0:16], 16) // 8 == lane[0:size, 0:16]
            table = info[slot]
        return dot(chosen.astype(F32).astype(BF), table).astype(BF)

    def attend(part, start, size):
        buf = (qg, kv)[part]
        where_at = place[start : start + size, :]
        if part == 0:
            where_at = where_at + shifts(start, size)
        at = dot(where_at, spread_ref[...])
        lr, lc = (lane_row, lane_col) if part == 0 else (aim_row, aim_col)
        gap = jnp.maximum(jnp.abs(at[:, 0:128] - lr), jnp.abs(at[:, 128:256] - lc))
        bias = jnp.where(gap <= 2.5, shift_open, 1e9)
        bias = jnp.concatenate([bias, bias], axis=1)
        for h in range(PAIRS):
            one = buf[start : start + size, 128 * h : 128 * h + 128]
            two = buf[start : start + size, 384 + 128 * h : 384 + 128 * h + 128]
            score = dot(one, bd[2 * part, h], ((1,), (1,)))
            dweight = dot(two, bd[2 * part + 1, h], ((1,), (1,)))
            e = jnp.exp(jnp.minimum(bias - score * 0.125, 88.0))
            sig = 1.0 / (1.0 + e)
            dscore = (dweight * (sig * (1.0 - sig))).astype(BF)
            acc[part, h] += dot(dscore, one, ((0,), (0,)))
            if part == 0:
                acc[2, h] += dot(sig.astype(BF), two, ((0,), (0,)))

    def gather(i, scale):
        parts = [jnp.where(low, acc[i, h, 0:128], acc[i, h, 128:256]) * scale for h in range(PAIRS)]
        return jnp.concatenate(parts, axis=1)

    attend(0, OWN, 128)
    attend(1, OWN, 128)
    cps["near", 2].wait_recv()
    for t in range(2):
        cps["near", t].wait_recv()
        attend(t, NEAR, 96)
    cps["right", 2].wait_recv()
    cps["left", 2].wait_recv()
    cps["fwd", 2] = send(
        info.at[pl.ds(I_SIDE, 2)], info.at[pl.ds(I_NSIDE, 2)], S_FWD + 2, near
    )

    def side(t, buf):
        cps["right", t].wait_recv()
        cps["left", t].wait_recv()
        cps["fwd", t] = send(buf.at[rng(SIDE)], buf.at[rng(NSIDE)], S_FWD + t, near)
        attend(t, SIDE, 96)

    side(0, qg)
    for name in ("far", "cr", "cl"):
        cps[name, 2].wait_recv()
    cps["far", 0].wait_recv()
    attend(0, FAR, 96)
    cps["fwd", 2].wait_recv()
    cps["fwd", 0].wait_recv()
    attend(0, NSIDE, 96)
    cps["cr", 0].wait_recv()
    cps["cl", 0].wait_recv()
    attend(0, CORNER, 96)

    dk = gather(0, 0.125).astype(BF)
    dv = (gather(2, 1.0) * key_open).astype(BF)
    dmine[1] = dk
    dmine[2] = dv
    cps["dkv"] = send(dmine.at[pl.ds(1, 2)], dother.at[pl.ds(1, 2)], S_DKV, near)
    cps["hx"].wait_recv()
    cps["dkv"].wait_recv()

    def partial(m, t):
        total = dot(hp[core, t], dmine[m], ((0,), (0,)))
        return total + dot(hx[t], dother[m], ((0,), (0,)))

    for m in (1, 2):
        w = partial(m, 1)
        for i in range(nx):
            piece = w[96 * i : 96 * i + 96]
            dw[i, :, 384 * m : 384 * m + 384] = piece
            xs_kv[i, :, 384 * (m - 1) : 384 * m] = piece.astype(BF)
    for v, d in x_peers:
        cps["xkv", d] = send(xs_kv.at[v], xr_kv.at[d - 1], S_X + d - 1, x_dev(v))
    side(1, kv)
    cps["far", 1].wait_recv()
    attend(1, FAR, 96)
    cps["fwd", 1].wait_recv()
    attend(1, NSIDE, 96)
    cps["cr", 1].wait_recv()
    cps["cl", 1].wait_recv()
    attend(1, CORNER, 96)
    dq = gather(1, 0.125).astype(BF)
    dmine[0] = dq
    cps["dq"] = send(dmine.at[0], dother.at[0], S_DQ, near)
    heg_ref[...] = dot(dq, wq_ref[...], ((1,), (1,))).astype(BF)
    cps["dq"].wait_recv()
    w = partial(0, 0)
    for i in range(nx):
        piece = w[96 * i : 96 * i + 96]
        dw[i, :, 0:384] = piece
        xs_q[i] = piece.astype(BF)
    for v, d in x_peers:
        cps["xq", d] = send(xs_q.at[v], xr_q.at[d - 1], S_X + 3 + d - 1, x_dev(v))
    ihcg_ref[...] = (
        dot(dk, wk_ref[...], ((1,), (1,))) + dot(dv, wv_ref[...], ((1,), (1,)))
    ).astype(BF)

    def to_y(dst, at, total):
        laid = dot(total.astype(BF), toy_ref[...]).astype(BF)
        for h in range(2):
            for l in range(4):
                dst[4 * h + l, :, 128 * at : 128 * at + 128] = laid[
                    48 * h : 48 * h + 48, 128 * l : 128 * l + 128
                ]

    for _, d in x_peers:
        cps["xkv", d].wait_recv()
    for m in (1, 2):
        total = dw[x, :, 384 * m : 384 * m + 384]
        for _, d in x_peers:
            total = total + xr_kv[d - 1, :, 384 * (m - 1) : 384 * m].astype(F32)
        to_y(ys_kv, m - 1, total)
    for v, d in y_peers:
        cps["ykv", d] = send(ys_kv.at[v], yr_kv.at[d - 1], S_YKV + d - 1, y_dev(v))
    for _, d in x_peers:
        cps["xq", d].wait_recv()
    total = dw[x, :, 0:384]
    for _, d in x_peers:
        total = total + xr_q[d - 1].astype(F32)
    to_y(ys_q, 0, total)
    for v, d in y_peers:
        cps["yq", d] = send(ys_q.at[v], yr_q.at[d - 1], S_YQ + d - 1, y_dev(v))
    total_kv = ys_kv[y].astype(F32)
    for _, d in y_peers:
        cps["ykv", d].wait_recv()
        total_kv = total_kv + yr_kv[d - 1].astype(F32)
    total_q = ys_q[y].astype(F32)
    for _, d in y_peers:
        cps["yq", d].wait_recv()
        total_q = total_q + yr_q[d - 1].astype(F32)
    total = jnp.concatenate([total_q, total_kv], axis=1)
    laid = dot(total.astype(BF), toz_ref[...]).astype(BF)
    for i in range(nz):
        zs[i] = laid[:, 128 * i : 128 * i + 128]
    for v, d in z_peers:
        cps["z", d] = send(zs.at[v], zr.at[d - 1], S_Z + d - 1, z_dev(v))
    total = zs[z].astype(F32)
    for _, d in z_peers:
        cps["z", d].wait_recv()
        total = total + zr[d - 1].astype(F32)
    total = total * (1.0 / math.sqrt(128.0 * rows * cols))
    for m in range(3):
        wg_ref[m] = total[:, 12 * m : 12 * m + 12]
    for cp in started:
        cp.wait_send()


def on_device(rows, cols, he, ihc, he_mask, ihc_mask, offsets, wq, wk, wv, grad_out):
    nx, nz = rows // 4, cols // 4
    vm = pl.BlockSpec(memory_space=pltpu.VMEM)
    consts = constants()
    args = (
        offsets,
        he.reshape(128, 768), ihc.reshape(128, 768),
        he_mask, ihc_mask,
        wq, wk, wv, grad_out.reshape(128, 384), *consts,
    )
    heg, ihcg, wg = pl.pallas_call(
        functools.partial(kernel, rows, cols),
        out_shape=(
            jax.ShapeDtypeStruct((128, 768), BF),
            jax.ShapeDtypeStruct((128, 768), BF),
            jax.ShapeDtypeStruct((3, 48, 12), F32),
        ),
        in_specs=[pl.BlockSpec(memory_space=pl.ANY)] * len(args),
        out_specs=(vm, vm, vm),
        scratch_shapes=[pltpu.VMEM(a.shape, a.dtype) for a in args]
        + [
            pltpu.SemaphoreType.DMA((len(args),)),
            pltpu.VMEM((ROWS, 768), BF),
            pltpu.VMEM((ROWS, 768), BF),
            pltpu.VMEM((96, 768), BF),
            pltpu.VMEM((96, 768), BF),
            pltpu.VMEM((I_ALL, 16, 128), BF),
            pltpu.VMEM((ROWS, 128), BF),
            pltpu.VMEM((4, PAIRS, 256, 128), BF),
            pltpu.VMEM((3, PAIRS, 256, 128), F32),
            pltpu.VMEM((2, 2, 128, 384), BF),
            pltpu.VMEM((2, 128, 384), BF),
            pltpu.VMEM((3, 128, 384), BF),
            pltpu.VMEM((3, 128, 384), BF),
            pltpu.VMEM((nx, 96, 1152), F32),
            pltpu.VMEM((nx, 96, 384), BF),
            pltpu.VMEM((nx - 1, 96, 384), BF),
            pltpu.VMEM((nx, 96, 768), BF),
            pltpu.VMEM((nx - 1, 96, 768), BF),
            pltpu.VMEM((8, 48, 128), BF),
            pltpu.VMEM((7, 48, 128), BF),
            pltpu.VMEM((8, 48, 256), BF),
            pltpu.VMEM((7, 48, 256), BF),
            pltpu.VMEM((nz, 48, 128), BF),
            pltpu.VMEM((nz - 1, 48, 128), BF),
            pltpu.SemaphoreType.DMA((S_ALL,)),
            pltpu.SemaphoreType.DMA((S_ALL,)),
        ],
        compiler_params=pltpu.CompilerParams(
            collective_id=0, has_side_effects=True, vmem_limit_bytes=56 << 20
        ),
    )(*args)
    return heg.reshape(8, 16, 768), ihcg.reshape(8, 16, 768), wg


def solution(mesh):
    placed = (
        P("row", "col", None), P("row", "col", None), P("row", "col"), P("row", "col"),
        P("row", "col", None), P(), P(), P(), P("row", "col", None),
    )
    return jax.shard_map(
        functools.partial(on_device, mesh.shape["row"], mesh.shape["col"]),
        mesh=mesh,
        in_specs=placed,
        out_specs=(P("row", "col", None), P("row", "col", None), P(None, "row", "col")),
        check_vma=False,
    )
```

```python
import functools
import math

import jax
import jax.numpy as jnp
import numpy as np
from jax import lax
from jax.experimental import pallas as pl
from jax.experimental.pallas import tpu as pltpu
from jax.sharding import PartitionSpec as P

MESH = pl.DeviceIdType.MESH
BF = jnp.bfloat16
F32 = jnp.float32
PAIRS = 3
OWN, NEAR, SIDE, NSIDE, FAR, CORNER, ROWS = 0, 128, 224, 320, 416, 512, 608
S_NEAR, S_FAR, S_RIGHT, S_LEFT, S_FWD, S_CR, S_CL = 0, 3, 6, 9, 12, 15, 18
S_HX, S_DKV, S_DQ, S_X, S_YKV, S_YQ, S_Z, S_ALL = 21, 22, 23, 24, 30, 37, 44, 51
I_OWN, I_NEAR, I_SIDE, I_NSIDE, I_FAR, I_CORNER, I_ALL = 0, 1, 2, 4, 6, 7, 9


def constants():
    n = np.arange(48)
    pack = np.zeros((96, 128), np.float32)
    pack[n, (n // 6) * 16 + 10 + n % 6] = 1
    pack[48 + n, (n // 6) * 16 + n % 6] = 1
    perm = np.zeros((768, 768), np.float32)
    f = np.arange(768)
    slab, inner = f // 48, f % 48
    perm[f, (slab % 2) * 384 + (slab // 2) * 48 + inner] = 1
    to_y = np.zeros((384, 512), np.float32)
    lane = np.arange(384)
    c, j = lane // 12, lane % 12
    to_y[lane, (c % 4) * 128 + (c // 4) * 12 + j] = 1
    to_z = np.zeros((384, 1024), np.float32)
    for part in range(3):
        k = np.arange(96)
        to_z[part * 128 + k, (k // 12) * 128 + part * 12 + k % 12] = 1
    spread = np.zeros((128, 256), np.float32)
    spread[0, :128] = 1
    spread[64, 128:] = 1
    place = np.zeros((2, ROWS, 128), np.float32)
    for core in range(2):
        near0, far0 = (8, -6) if core == 0 else (-6, 8)
        own = np.arange(128)
        row, col = np.zeros(ROWS), np.zeros(ROWS)
        row[:128], col[:128] = own // 16, own % 16
        w = np.arange(96)
        row[NEAR : NEAR + 96], col[NEAR : NEAR + 96] = near0 + w // 16, w % 16
        row[FAR : FAR + 96], col[FAR : FAR + 96] = far0 + w // 16, w % 16
        s = w % 48
        scol = np.where(w < 48, -6 + s % 6, 16 + s % 6)
        row[SIDE : SIDE + 96], col[SIDE : SIDE + 96] = s // 6, scol
        row[NSIDE : NSIDE + 96] = (8 if core == 0 else -8) + s // 6
        col[NSIDE : NSIDE + 96] = scol
        row[CORNER : CORNER + 96] = (-8 if core == 0 else 8) + s // 6
        col[CORNER : CORNER + 96] = scol
        place[core, :, 0] = row
        place[core, :, 64] = col
    return [jnp.asarray(a, BF) for a in (pack, perm, to_y, to_z, spread, place)]


def dot(a, b, dims=((1,), (0,))):
    return lax.dot_general(a, b, (dims, ((), ())), preferred_element_type=F32)


def kernel(
    rows, cols,
    off_in, he_in, ihc_in, hm_in, im_in, wq_in, wk_in, wv_in, g_in,
    pack_in, perm_in, toy_in, toz_in, spread_in, place_in,
    heg_ref, ihcg_ref, wg_ref,
    off_ref, he_ref, ihc_ref, hm_ref, im_ref, wq_ref, wk_ref, wv_ref, g_ref,
    pack_ref, perm_ref, toy_ref, toz_ref, spread_ref, place_ref, in_sem,
    qg, kv, pq, info, place, bd, acc, dqp, dqr, dqn, side_sum, dqa, hp, hx, dmine, dother, dw,
    xs_q, xr_q, xs_kv, xr_kv, ys_q, yr_q, ys_kv, yr_kv, zs, zr, send_sem, recv_sem,
):
    r, c = lax.axis_index("row"), lax.axis_index("col")
    x, yh, core = r // 4, lax.rem(r // 2, 2), lax.rem(r, 2)
    z, yl = c // 4, lax.rem(c, 4)
    y = yh * 4 + yl
    nx, nz = rows // 4, cols // 4
    near = (r + 1 - 2 * core, c)
    far = (lax.rem(r + 2 * core - 1 + rows, rows), c)
    right = (r, lax.rem(c + 1, cols))
    left = (r, lax.rem(c + cols - 1, cols))
    far_right, far_left = (far[0], right[1]), (far[0], left[1])
    x_peers = [(lax.rem(x + d, nx), d) for d in range(1, nx)]
    y_peers = [(lax.rem(y + d, 8), d) for d in range(1, 8)]
    z_peers = [(lax.rem(z + d, nz), d) for d in range(1, nz)]

    def x_dev(v):
        return (v * 4 + yh * 2 + core, c)

    def y_dev(v):
        return (x * 4 + (v // 4) * 2 + core, z * 4 + lax.rem(v, 4))

    def z_dev(v):
        return (r, v * 4 + yl)

    partners = [near, far, right, left, far_right, far_left]
    partners += [x_dev(v) for v, _ in x_peers]
    partners += [y_dev(v) for v, _ in y_peers]
    partners += [z_dev(v) for v, _ in z_peers]
    barrier = pltpu.get_barrier_semaphore()
    for dev in partners:
        pl.semaphore_signal(barrier, inc=1, device_id=dev, device_id_type=MESH)

    loads = {}
    order = (
        (he_in, he_ref), (wq_in, wq_ref), (g_in, g_ref), (hm_in, hm_ref), (off_in, off_ref),
        (pack_in, pack_ref), (ihc_in, ihc_ref), (wk_in, wk_ref), (wv_in, wv_ref),
        (im_in, im_ref), (perm_in, perm_ref), (place_in, place_ref), (spread_in, spread_ref),
        (toy_in, toy_ref), (toz_in, toz_ref),
    )
    for i, (src, dst) in enumerate(order):
        loads[i] = pltpu.make_async_copy(src, dst, in_sem.at[i])
    for i in range(6):
        loads[i].start()

    def ready(*which):
        for i in which:
            loads[i].wait()

    started = []

    def send(src, dst, sem, dev):
        cp = pltpu.make_async_remote_copy(
            src_ref=src, dst_ref=dst, send_sem=send_sem.at[sem], recv_sem=recv_sem.at[sem],
            device_id=dev, device_id_type=MESH,
        )
        cp.start()
        started.append(cp)
        return cp

    tile = lax.broadcasted_iota(jnp.int32, (128, 128), 0)
    lane = lax.broadcasted_iota(jnp.int32, (128, 128), 1)

    def column(mask):
        mine = (tile[:, 0:8] // 16 == lane[:, 0:8]).astype(F32)
        spread = dot(mine, mask.astype(F32))
        here = lax.rem(tile[:, 0:16], 16) == lane[:, 0:16]
        return jnp.sum(jnp.where(here, spread, 0.0), axis=1, keepdims=True)

    ready(0, 1)
    for i in range(6, len(order)):
        loads[i].start()
    q = dot(he_ref[...], wq_ref[...]).astype(BF)
    qg[0:128, 0:384] = q
    ready(2, 3, 4, 5)
    qg[0:128, 384:768] = (g_ref[...].astype(F32) * column(hm_ref[...])).astype(BF)
    off = off_ref[0].astype(F32)
    a0, b0, a1, b1 = off[0:1, 0:1], off[0:1, 1:2], off[1:2, 0:1], off[1:2, 1:2]
    block = jnp.where(lane < 64, jnp.where(tile == 0, a0, a1), jnp.where(tile == 0, b0, b1))
    info[I_OWN] = block[0:16].astype(BF)
    pq[...] = dot(pack_ref[...], qg[0:128, :]).astype(BF)
    pl.semaphore_wait(barrier, len(partners))

    near_at = pl.ds(pl.multiple_of(32 * (1 - core), 32), 96)
    far_at = pl.ds(pl.multiple_of(32 * core, 32), 96)

    def rng(start, size=96):
        return pl.ds(start, size)

    cps = {}
    own_info = info.at[I_OWN]
    cps["far", 2] = send(own_info, info.at[I_FAR], S_FAR + 2, far)
    cps["near", 2] = send(own_info, info.at[I_NEAR], S_NEAR + 2, near)
    cps["right", 2] = send(own_info, info.at[I_SIDE], S_RIGHT + 2, right)
    cps["left", 2] = send(own_info, info.at[I_SIDE + 1], S_LEFT + 2, left)
    cps["cr", 2] = send(own_info, info.at[I_CORNER], S_CR + 2, far_right)
    cps["cl", 2] = send(own_info, info.at[I_CORNER + 1], S_CL + 2, far_left)
    to_right, to_left = pq.at[rng(0, 48)], pq.at[rng(48, 48)]
    cps["far", 0] = send(qg.at[far_at], qg.at[rng(FAR)], S_FAR, far)
    cps["cr", 0] = send(to_right, qg.at[rng(CORNER, 48)], S_CR, far_right)
    cps["cl", 0] = send(to_left, qg.at[rng(CORNER + 48, 48)], S_CL, far_left)
    cps["right", 0] = send(to_right, qg.at[rng(SIDE, 48)], S_RIGHT, right)
    cps["left", 0] = send(to_left, qg.at[rng(SIDE + 48, 48)], S_LEFT, left)
    cps["near", 0] = send(qg.at[near_at], qg.at[rng(NEAR)], S_NEAR, near)

    ready(6, 7, 8, 9)
    ihc = ihc_ref[...]
    key_open = column(im_ref[...])
    kv[0:128, 0:384] = (dot(ihc, wk_ref[...]) * key_open).astype(BF)
    kv[0:128, 384:768] = (dot(ihc, wv_ref[...]) * key_open).astype(BF)

    ready(*range(10, 15))
    for t, ref in enumerate((he_ref, ihc_ref)):
        ordered = dot(ref[...], perm_ref[...]).astype(BF)
        hp[0, t] = ordered[:, 0:384]
        hp[1, t] = ordered[:, 384:768]
    cps["hx"] = send(hp.at[1 - core], hx, S_HX, near)

    place[...] = place_ref[core]
    row_bad = jnp.where(core == 0, (r == 0).astype(F32), (r == rows - 1).astype(F32)) * 1024.0
    left_bad = (c == 0).astype(F32) * 1024.0
    right_bad = (c == cols - 1).astype(F32) * 1024.0

    def shift(start, size, amount):
        place[start : start + size, :] = (
            place[start : start + size, :].astype(F32) + amount
        ).astype(BF)

    for base in (SIDE, NSIDE):
        shift(base, 48, left_bad)
        shift(base + 48, 48, right_bad)
    shift(FAR, 96, row_bad)
    shift(CORNER, 48, left_bad + row_bad)
    shift(CORNER + 48, 48, right_bad + row_bad)

    low = lane < 64
    zero = jnp.zeros((128, 128), BF)
    for i, base in enumerate((0, 384)):
        for h in range(PAIRS):
            part = kv[0:128, base + 128 * h : base + 128 * h + 128]
            bd[i, h, 0:128, :] = jnp.where(low, part, zero)
            bd[i, h, 128:256, :] = jnp.where(low, zero, part)
    acc[...] = jnp.zeros(acc.shape, F32)

    vec = lax.broadcasted_iota(jnp.int32, (1, 128), 1)
    lane_row = (vec // 16).astype(F32)
    lane_col = lax.rem(vec, 16).astype(F32)
    shift_open = math.log(25.0)

    slots = {NEAR: I_NEAR, SIDE: I_SIDE, NSIDE: I_NSIDE, FAR: I_FAR, CORNER: I_CORNER}

    def shifts(start, size):
        slot = slots.get(start, I_OWN)
        if start in (SIDE, NSIDE, CORNER):
            chosen = jnp.where(tile[0:size, 0:32] < 48, 1, 16) == lane[0:size, 0:32]
            table = jnp.concatenate([info[slot], info[slot + 1]], axis=0)
        else:
            chosen = lax.rem(tile[0:size, 0:16], 16) // 8 == lane[0:size, 0:16]
            table = info[slot]
        return dot(chosen.astype(F32).astype(BF), table).astype(BF)

    def attend(start, size):
        where_at = place[start : start + size, :] + shifts(start, size)
        at = dot(where_at, spread_ref[...])
        gap = jnp.maximum(jnp.abs(at[:, 0:128] - lane_row), jnp.abs(at[:, 128:256] - lane_col))
        bias = jnp.where(gap <= 2.5, shift_open, 1e9)
        bias = jnp.concatenate([bias, bias], axis=1)
        for h in range(PAIRS):
            one = qg[start : start + size, 128 * h : 128 * h + 128]
            two = qg[start : start + size, 384 + 128 * h : 384 + 128 * h + 128]
            score = dot(one, bd[0, h], ((1,), (1,)))
            dweight = dot(two, bd[1, h], ((1,), (1,)))
            e = jnp.exp(jnp.minimum(bias - score * 0.125, 88.0))
            sig = 1.0 / (1.0 + e)
            dscore = (dweight * (sig * (1.0 - sig))).astype(BF)
            acc[0, h] += dot(dscore, one, ((0,), (0,)))
            acc[1, h] += dot(sig.astype(BF), two, ((0,), (0,)))
            back = dot(dscore, bd[0, h]) * 0.125
            dqp[start : start + size, 128 * h : 128 * h + 128] = back.astype(BF)

    def gather(i, scale):
        parts = [jnp.where(low, acc[i, h, 0:128], acc[i, h, 128:256]) * scale for h in range(PAIRS)]
        return jnp.concatenate(parts, axis=1)

    attend(OWN, 128)
    cps["near", 2].wait_recv()
    cps["near", 0].wait_recv()
    attend(NEAR, 96)
    cps["near", 1] = send(dqp.at[rng(NEAR)], dqr.at[rng(NEAR)], S_NEAR + 1, near)
    for name in ("right", "left"):
        cps[name, 2].wait_recv()
        cps[name, 0].wait_recv()
    cps["fwd", 2] = send(
        info.at[pl.ds(I_SIDE, 2)], info.at[pl.ds(I_NSIDE, 2)], S_FWD + 2, near
    )
    cps["fwd", 0] = send(qg.at[rng(SIDE)], qg.at[rng(NSIDE)], S_FWD, near)
    attend(SIDE, 96)
    cps["far", 2].wait_recv()
    cps["far", 0].wait_recv()
    attend(FAR, 96)
    cps["far", 1] = send(dqp.at[rng(FAR)], dqr.at[rng(FAR)], S_FAR + 1, far)
    cps["fwd", 2].wait_recv()
    cps["fwd", 0].wait_recv()
    attend(NSIDE, 96)
    cps["fwd", 1] = send(dqp.at[rng(NSIDE)], dqn, S_FWD + 1, near)
    for name in ("cr", "cl"):
        cps[name, 2].wait_recv()
        cps[name, 0].wait_recv()
    attend(CORNER, 96)
    cps["cr", 1] = send(dqp.at[rng(CORNER, 48)], dqr.at[rng(CORNER, 48)], S_CR + 1, far_left)
    cps["cl", 1] = send(
        dqp.at[rng(CORNER + 48, 48)], dqr.at[rng(CORNER + 48, 48)], S_CL + 1, far_right
    )
    cps["fwd", 1].wait_recv()
    side_sum[...] = (dqp[SIDE : SIDE + 96, :].astype(F32) + dqn[...].astype(F32)).astype(BF)
    cps["right", 1] = send(side_sum.at[rng(0, 48)], dqr.at[rng(SIDE, 48)], S_RIGHT + 1, left)
    cps["left", 1] = send(
        side_sum.at[rng(48, 48)], dqr.at[rng(SIDE + 48, 48)], S_LEFT + 1, right
    )

    dk = gather(0, 0.125).astype(BF)
    dv = (gather(1, 1.0) * key_open).astype(BF)
    dmine[1] = dk
    dmine[2] = dv
    cps["dkv"] = send(dmine.at[pl.ds(1, 2)], dother.at[pl.ds(1, 2)], S_DKV, near)
    cps["hx"].wait_recv()
    cps["dkv"].wait_recv()

    def partial(m, t):
        total = dot(hp[core, t], dmine[m], ((0,), (0,)))
        return total + dot(hx[t], dother[m], ((0,), (0,)))

    for m in (1, 2):
        w = partial(m, 1)
        for i in range(nx):
            piece = w[96 * i : 96 * i + 96]
            dw[i, :, 384 * m : 384 * m + 384] = piece
            xs_kv[i, :, 384 * (m - 1) : 384 * m] = piece.astype(BF)
    for v, d in x_peers:
        cps["xkv", d] = send(xs_kv.at[v], xr_kv.at[d - 1], S_X + d - 1, x_dev(v))
    ihcg_ref[...] = (
        dot(dk, wk_ref[...], ((1,), (1,))) + dot(dv, wv_ref[...], ((1,), (1,)))
    ).astype(BF)
    dqa[...] = dqp[0:128, :].astype(F32)
    cps["near", 1].wait_recv()
    dqa[near_at, :] += dqr[NEAR : NEAR + 96, :].astype(F32)
    for name in ("far", "cr", "cl", "right", "left"):
        cps[name, 1].wait_recv()
    dqa[far_at, :] += dqr[FAR : FAR + 96, :].astype(F32)
    edges = dot(pack_ref[...], dqr[SIDE : SIDE + 96, :], ((0,), (0,)))
    edges = edges + dot(pack_ref[...], dqr[CORNER : CORNER + 96, :], ((0,), (0,)))
    dq = (dqa[...] + edges).astype(BF)
    dmine[0] = dq
    cps["dq"] = send(dmine.at[0], dother.at[0], S_DQ, near)
    heg_ref[...] = dot(dq, wq_ref[...], ((1,), (1,))).astype(BF)
    cps["dq"].wait_recv()
    w = partial(0, 0)
    for i in range(nx):
        piece = w[96 * i : 96 * i + 96]
        dw[i, :, 0:384] = piece
        xs_q[i] = piece.astype(BF)
    for v, d in x_peers:
        cps["xq", d] = send(xs_q.at[v], xr_q.at[d - 1], S_X + 3 + d - 1, x_dev(v))
    def to_y(dst, at, total):
        laid = dot(total.astype(BF), toy_ref[...]).astype(BF)
        for h in range(2):
            for l in range(4):
                dst[4 * h + l, :, 128 * at : 128 * at + 128] = laid[
                    48 * h : 48 * h + 48, 128 * l : 128 * l + 128
                ]

    for _, d in x_peers:
        cps["xkv", d].wait_recv()
    for m in (1, 2):
        total = dw[x, :, 384 * m : 384 * m + 384]
        for _, d in x_peers:
            total = total + xr_kv[d - 1, :, 384 * (m - 1) : 384 * m].astype(F32)
        to_y(ys_kv, m - 1, total)
    for v, d in y_peers:
        cps["ykv", d] = send(ys_kv.at[v], yr_kv.at[d - 1], S_YKV + d - 1, y_dev(v))
    for _, d in x_peers:
        cps["xq", d].wait_recv()
    total = dw[x, :, 0:384]
    for _, d in x_peers:
        total = total + xr_q[d - 1].astype(F32)
    to_y(ys_q, 0, total)
    for v, d in y_peers:
        cps["yq", d] = send(ys_q.at[v], yr_q.at[d - 1], S_YQ + d - 1, y_dev(v))
    total_kv = ys_kv[y].astype(F32)
    for _, d in y_peers:
        cps["ykv", d].wait_recv()
        total_kv = total_kv + yr_kv[d - 1].astype(F32)
    total_q = ys_q[y].astype(F32)
    for _, d in y_peers:
        cps["yq", d].wait_recv()
        total_q = total_q + yr_q[d - 1].astype(F32)
    total = jnp.concatenate([total_q, total_kv], axis=1)
    laid = dot(total.astype(BF), toz_ref[...]).astype(BF)
    for i in range(nz):
        zs[i] = laid[:, 128 * i : 128 * i + 128]
    for v, d in z_peers:
        cps["z", d] = send(zs.at[v], zr.at[d - 1], S_Z + d - 1, z_dev(v))
    total = zs[z].astype(F32)
    for _, d in z_peers:
        cps["z", d].wait_recv()
        total = total + zr[d - 1].astype(F32)
    total = total * (1.0 / math.sqrt(128.0 * rows * cols))
    for m in range(3):
        wg_ref[m] = total[:, 12 * m : 12 * m + 12]
    for cp in started:
        cp.wait_send()


def on_device(rows, cols, he, ihc, he_mask, ihc_mask, offsets, wq, wk, wv, grad_out):
    nx, nz = rows // 4, cols // 4
    vm = pl.BlockSpec(memory_space=pltpu.VMEM)
    consts = constants()
    args = (
        offsets,
        he.reshape(128, 768), ihc.reshape(128, 768),
        he_mask, ihc_mask,
        wq, wk, wv, grad_out.reshape(128, 384), *consts,
    )
    heg, ihcg, wg = pl.pallas_call(
        functools.partial(kernel, rows, cols),
        out_shape=(
            jax.ShapeDtypeStruct((128, 768), BF),
            jax.ShapeDtypeStruct((128, 768), BF),
            jax.ShapeDtypeStruct((3, 48, 12), F32),
        ),
        in_specs=[pl.BlockSpec(memory_space=pl.ANY)] * len(args),
        out_specs=(vm, vm, vm),
        scratch_shapes=[pltpu.VMEM(a.shape, a.dtype) for a in args]
        + [
            pltpu.SemaphoreType.DMA((len(args),)),
            pltpu.VMEM((ROWS, 768), BF),
            pltpu.VMEM((128, 768), BF),
            pltpu.VMEM((96, 768), BF),
            pltpu.VMEM((I_ALL, 16, 128), BF),
            pltpu.VMEM((ROWS, 128), BF),
            pltpu.VMEM((2, PAIRS, 256, 128), BF),
            pltpu.VMEM((2, PAIRS, 256, 128), F32),
            pltpu.VMEM((ROWS, 384), BF),
            pltpu.VMEM((ROWS, 384), BF),
            pltpu.VMEM((96, 384), BF),
            pltpu.VMEM((96, 384), BF),
            pltpu.VMEM((128, 384), F32),
            pltpu.VMEM((2, 2, 128, 384), BF),
            pltpu.VMEM((2, 128, 384), BF),
            pltpu.VMEM((3, 128, 384), BF),
            pltpu.VMEM((3, 128, 384), BF),
            pltpu.VMEM((nx, 96, 1152), F32),
            pltpu.VMEM((nx, 96, 384), BF),
            pltpu.VMEM((nx - 1, 96, 384), BF),
            pltpu.VMEM((nx, 96, 768), BF),
            pltpu.VMEM((nx - 1, 96, 768), BF),
            pltpu.VMEM((8, 48, 128), BF),
            pltpu.VMEM((7, 48, 128), BF),
            pltpu.VMEM((8, 48, 256), BF),
            pltpu.VMEM((7, 48, 256), BF),
            pltpu.VMEM((nz, 48, 128), BF),
            pltpu.VMEM((nz - 1, 48, 128), BF),
            pltpu.SemaphoreType.DMA((S_ALL,)),
            pltpu.SemaphoreType.DMA((S_ALL,)),
        ],
        compiler_params=pltpu.CompilerParams(
            collective_id=0, has_side_effects=True, vmem_limit_bytes=56 << 20
        ),
    )(*args)
    return heg.reshape(8, 16, 768), ihcg.reshape(8, 16, 768), wg


def solution(mesh):
    placed = (
        P("row", "col", None), P("row", "col", None), P("row", "col"), P("row", "col"),
        P("row", "col", None), P(), P(), P(), P("row", "col", None),
    )
    return jax.shard_map(
        functools.partial(on_device, mesh.shape["row"], mesh.shape["col"]),
        mesh=mesh,
        in_specs=placed,
        out_specs=(P("row", "col", None), P("row", "col", None), P(None, "row", "col")),
        check_vma=False,
    )
```

```python
import functools
import math

import jax
import jax.numpy as jnp
import numpy as np
from jax import lax
from jax.experimental import pallas as pl
from jax.experimental.pallas import tpu as pltpu
from jax.sharding import PartitionSpec as P

MESH = pl.DeviceIdType.MESH
BF = jnp.bfloat16
F32 = jnp.float32
PAIRS = 3
OWN, NEAR, SIDE, NSIDE, FAR, CORNER, ROWS = 0, 128, 224, 320, 416, 512, 608
S_NEAR, S_FAR, S_RIGHT, S_LEFT, S_FWD, S_CR, S_CL = 0, 3, 6, 9, 12, 15, 18
S_HX, S_DKV, S_DQ, S_X, S_YKV, S_YQ, S_Z, S_ALL = 21, 22, 23, 24, 30, 37, 44, 51
I_OWN, I_NEAR, I_SIDE, I_NSIDE, I_FAR, I_CORNER, I_ALL = 0, 1, 2, 4, 6, 7, 9


def constants():
    n = np.arange(48)
    pack = np.zeros((96, 128), np.float32)
    pack[n, (n // 6) * 16 + 10 + n % 6] = 1
    pack[48 + n, (n // 6) * 16 + n % 6] = 1
    perm = np.zeros((768, 768), np.float32)
    f = np.arange(768)
    slab, inner = f // 48, f % 48
    perm[f, (slab % 2) * 384 + (slab // 2) * 48 + inner] = 1
    to_y = np.zeros((384, 512), np.float32)
    lane = np.arange(384)
    c, j = lane // 12, lane % 12
    to_y[lane, (c % 4) * 128 + (c // 4) * 12 + j] = 1
    to_z = np.zeros((384, 1024), np.float32)
    for part in range(3):
        k = np.arange(96)
        to_z[part * 128 + k, (k // 12) * 128 + part * 12 + k % 12] = 1
    spread = np.zeros((128, 256), np.float32)
    spread[0, :128] = 1
    spread[64, 128:] = 1
    place = np.zeros((2, ROWS, 128), np.float32)
    for core in range(2):
        near0, far0 = (8, -6) if core == 0 else (-6, 8)
        own = np.arange(128)
        row, col = np.zeros(ROWS), np.zeros(ROWS)
        row[:128], col[:128] = own // 16, own % 16
        w = np.arange(96)
        row[NEAR : NEAR + 96], col[NEAR : NEAR + 96] = near0 + w // 16, w % 16
        row[FAR : FAR + 96], col[FAR : FAR + 96] = far0 + w // 16, w % 16
        s = w % 48
        scol = np.where(w < 48, -6 + s % 6, 16 + s % 6)
        row[SIDE : SIDE + 96], col[SIDE : SIDE + 96] = s // 6, scol
        row[NSIDE : NSIDE + 96] = (8 if core == 0 else -8) + s // 6
        col[NSIDE : NSIDE + 96] = scol
        row[CORNER : CORNER + 96] = (-8 if core == 0 else 8) + s // 6
        col[CORNER : CORNER + 96] = scol
        place[core, :, 0] = row
        place[core, :, 64] = col
    return [jnp.asarray(a, BF) for a in (pack, perm, to_y, to_z, spread, place)]


def dot(a, b, dims=((1,), (0,))):
    return lax.dot_general(a, b, (dims, ((), ())), preferred_element_type=F32)


def kernel(
    rows, cols,
    off_in, he_in, ihc_in, hm_in, im_in, wq_in, wk_in, wv_in, g_in,
    pack_in, perm_in, toy_in, toz_in, spread_in, place_in,
    heg_out, ihcg_out, wg_out,
    heg_ref, ihcg_ref, wg_ref, out_sem,
    off_ref, he_ref, ihc_ref, hm_ref, im_ref, wq_ref, wk_ref, wv_ref, g_ref,
    pack_ref, perm_ref, toy_ref, toz_ref, spread_ref, place_ref, in_sem,
    qg, kv, pq, info, place, bd, acc, dqp, dqr, dqn, side_sum, dqa, hp, hx, dmine, dother, dw,
    xs_q, xr_q, xs_kv, xr_kv, ys_q, yr_q, ys_kv, yr_kv, zs, zr, send_sem, recv_sem,
):
    r, c = lax.axis_index("row"), lax.axis_index("col")
    x, yh, core = r // 4, lax.rem(r // 2, 2), lax.rem(r, 2)
    z, yl = c // 4, lax.rem(c, 4)
    y = yh * 4 + yl
    nx, nz = rows // 4, cols // 4
    near = (r + 1 - 2 * core, c)
    far = (lax.rem(r + 2 * core - 1 + rows, rows), c)
    right = (r, lax.rem(c + 1, cols))
    left = (r, lax.rem(c + cols - 1, cols))
    far_right, far_left = (far[0], right[1]), (far[0], left[1])
    x_peers = [(lax.rem(x + d, nx), d) for d in range(1, nx)]
    y_peers = [(lax.rem(y + d, 8), d) for d in range(1, 8)]
    z_peers = [(lax.rem(z + d, nz), d) for d in range(1, nz)]

    def x_dev(v):
        return (v * 4 + yh * 2 + core, c)

    def y_dev(v):
        return (x * 4 + (v // 4) * 2 + core, z * 4 + lax.rem(v, 4))

    def z_dev(v):
        return (r, v * 4 + yl)

    partners = [near, far, right, left, far_right, far_left]
    partners += [x_dev(v) for v, _ in x_peers]
    partners += [y_dev(v) for v, _ in y_peers]
    partners += [z_dev(v) for v, _ in z_peers]
    barrier = pltpu.get_barrier_semaphore()
    for dev in partners:
        pl.semaphore_signal(barrier, inc=1, device_id=dev, device_id_type=MESH)

    loads = {}
    order = (
        (he_in, he_ref), (wq_in, wq_ref), (g_in, g_ref), (hm_in, hm_ref), (off_in, off_ref),
        (pack_in, pack_ref), (ihc_in, ihc_ref), (wk_in, wk_ref), (wv_in, wv_ref),
        (im_in, im_ref), (perm_in, perm_ref), (place_in, place_ref), (spread_in, spread_ref),
        (toy_in, toy_ref), (toz_in, toz_ref),
    )
    for i, (src, dst) in enumerate(order):
        loads[i] = pltpu.make_async_copy(src, dst, in_sem.at[i])
    for i in range(6):
        loads[i].start()

    def ready(*which):
        for i in which:
            loads[i].wait()

    outs = []

    def leave(i, src, dst):
        cp = pltpu.make_async_copy(src, dst, out_sem.at[i])
        cp.start()
        outs.append(cp)

    started = []

    def send(src, dst, sem, dev):
        cp = pltpu.make_async_remote_copy(
            src_ref=src, dst_ref=dst, send_sem=send_sem.at[sem], recv_sem=recv_sem.at[sem],
            device_id=dev, device_id_type=MESH,
        )
        cp.start()
        started.append(cp)
        return cp

    tile = lax.broadcasted_iota(jnp.int32, (128, 128), 0)
    lane = lax.broadcasted_iota(jnp.int32, (128, 128), 1)

    def column(mask):
        mine = (tile[:, 0:8] // 16 == lane[:, 0:8]).astype(F32)
        spread = dot(mine, mask.astype(F32))
        here = lax.rem(tile[:, 0:16], 16) == lane[:, 0:16]
        return jnp.sum(jnp.where(here, spread, 0.0), axis=1, keepdims=True)

    ready(0, 1)
    for i in range(6, len(order)):
        loads[i].start()
    q = dot(he_ref[...], wq_ref[...]).astype(BF)
    qg[0:128, 0:384] = q
    ready(2, 3, 4, 5)
    qg[0:128, 384:768] = (g_ref[...].astype(F32) * column(hm_ref[...])).astype(BF)
    off = off_ref[0].astype(F32)
    a0, b0, a1, b1 = off[0:1, 0:1], off[0:1, 1:2], off[1:2, 0:1], off[1:2, 1:2]
    block = jnp.where(lane < 64, jnp.where(tile == 0, a0, a1), jnp.where(tile == 0, b0, b1))
    info[I_OWN] = block[0:16].astype(BF)
    pq[...] = dot(pack_ref[...], qg[0:128, :]).astype(BF)
    pl.semaphore_wait(barrier, len(partners))

    near_at = pl.ds(pl.multiple_of(32 * (1 - core), 32), 96)
    far_at = pl.ds(pl.multiple_of(32 * core, 32), 96)

    def rng(start, size=96):
        return pl.ds(start, size)

    cps = {}
    own_info = info.at[I_OWN]
    cps["far", 2] = send(own_info, info.at[I_FAR], S_FAR + 2, far)
    cps["near", 2] = send(own_info, info.at[I_NEAR], S_NEAR + 2, near)
    cps["right", 2] = send(own_info, info.at[I_SIDE], S_RIGHT + 2, right)
    cps["left", 2] = send(own_info, info.at[I_SIDE + 1], S_LEFT + 2, left)
    cps["cr", 2] = send(own_info, info.at[I_CORNER], S_CR + 2, far_right)
    cps["cl", 2] = send(own_info, info.at[I_CORNER + 1], S_CL + 2, far_left)
    to_right, to_left = pq.at[rng(0, 48)], pq.at[rng(48, 48)]
    cps["far", 0] = send(qg.at[far_at], qg.at[rng(FAR)], S_FAR, far)
    cps["cr", 0] = send(to_right, qg.at[rng(CORNER, 48)], S_CR, far_right)
    cps["cl", 0] = send(to_left, qg.at[rng(CORNER + 48, 48)], S_CL, far_left)
    cps["right", 0] = send(to_right, qg.at[rng(SIDE, 48)], S_RIGHT, right)
    cps["left", 0] = send(to_left, qg.at[rng(SIDE + 48, 48)], S_LEFT, left)
    cps["near", 0] = send(qg.at[near_at], qg.at[rng(NEAR)], S_NEAR, near)

    ready(6, 7, 8, 9)
    ihc = ihc_ref[...]
    key_open = column(im_ref[...])
    kv[0:128, 0:384] = (dot(ihc, wk_ref[...]) * key_open).astype(BF)
    kv[0:128, 384:768] = (dot(ihc, wv_ref[...]) * key_open).astype(BF)

    ready(*range(10, 15))
    for t, ref in enumerate((he_ref, ihc_ref)):
        ordered = dot(ref[...], perm_ref[...]).astype(BF)
        hp[0, t] = ordered[:, 0:384]
        hp[1, t] = ordered[:, 384:768]
    cps["hx"] = send(hp.at[1 - core], hx, S_HX, near)

    place[...] = place_ref[core]
    row_bad = jnp.where(core == 0, (r == 0).astype(F32), (r == rows - 1).astype(F32)) * 1024.0
    left_bad = (c == 0).astype(F32) * 1024.0
    right_bad = (c == cols - 1).astype(F32) * 1024.0

    def shift(start, size, amount):
        place[start : start + size, :] = (
            place[start : start + size, :].astype(F32) + amount
        ).astype(BF)

    for base in (SIDE, NSIDE):
        shift(base, 48, left_bad)
        shift(base + 48, 48, right_bad)
    shift(FAR, 96, row_bad)
    shift(CORNER, 48, left_bad + row_bad)
    shift(CORNER + 48, 48, right_bad + row_bad)

    low = lane < 64
    zero = jnp.zeros((128, 128), BF)
    for i, base in enumerate((0, 384)):
        for h in range(PAIRS):
            part = kv[0:128, base + 128 * h : base + 128 * h + 128]
            bd[i, h, 0:128, :] = jnp.where(low, part, zero)
            bd[i, h, 128:256, :] = jnp.where(low, zero, part)
    acc[...] = jnp.zeros(acc.shape, F32)

    vec = lax.broadcasted_iota(jnp.int32, (1, 128), 1)
    lane_row = (vec // 16).astype(F32)
    lane_col = lax.rem(vec, 16).astype(F32)
    shift_open = math.log(25.0)

    slots = {NEAR: I_NEAR, SIDE: I_SIDE, NSIDE: I_NSIDE, FAR: I_FAR, CORNER: I_CORNER}

    def shifts(start, size):
        slot = slots.get(start, I_OWN)
        if start in (SIDE, NSIDE, CORNER):
            chosen = jnp.where(tile[0:size, 0:32] < 48, 1, 16) == lane[0:size, 0:32]
            table = jnp.concatenate([info[slot], info[slot + 1]], axis=0)
        else:
            chosen = lax.rem(tile[0:size, 0:16], 16) // 8 == lane[0:size, 0:16]
            table = info[slot]
        return dot(chosen.astype(F32).astype(BF), table).astype(BF)

    def attend(start, size):
        where_at = place[start : start + size, :] + shifts(start, size)
        at = dot(where_at, spread_ref[...])
        gap = jnp.maximum(jnp.abs(at[:, 0:128] - lane_row), jnp.abs(at[:, 128:256] - lane_col))
        bias = jnp.where(gap <= 2.5, shift_open, 1e9)
        bias = jnp.concatenate([bias, bias], axis=1)
        for h in range(PAIRS):
            one = qg[start : start + size, 128 * h : 128 * h + 128]
            two = qg[start : start + size, 384 + 128 * h : 384 + 128 * h + 128]
            score = dot(one, bd[0, h], ((1,), (1,)))
            dweight = dot(two, bd[1, h], ((1,), (1,)))
            e = jnp.exp(jnp.minimum(bias - score * 0.125, 88.0))
            sig = 1.0 / (1.0 + e)
            dscore = (dweight * (sig * (1.0 - sig))).astype(BF)
            acc[0, h] += dot(dscore, one, ((0,), (0,)))
            acc[1, h] += dot(sig.astype(BF), two, ((0,), (0,)))
            back = dot(dscore, bd[0, h]) * 0.125
            dqp[start : start + size, 128 * h : 128 * h + 128] = back.astype(BF)

    def gather(i, scale):
        parts = [jnp.where(low, acc[i, h, 0:128], acc[i, h, 128:256]) * scale for h in range(PAIRS)]
        return jnp.concatenate(parts, axis=1)

    attend(OWN, 128)
    cps["near", 2].wait_recv()
    cps["near", 0].wait_recv()
    attend(NEAR, 96)
    cps["near", 1] = send(dqp.at[rng(NEAR)], dqr.at[rng(NEAR)], S_NEAR + 1, near)
    for name in ("right", "left"):
        cps[name, 2].wait_recv()
        cps[name, 0].wait_recv()
    cps["fwd", 2] = send(
        info.at[pl.ds(I_SIDE, 2)], info.at[pl.ds(I_NSIDE, 2)], S_FWD + 2, near
    )
    cps["fwd", 0] = send(qg.at[rng(SIDE)], qg.at[rng(NSIDE)], S_FWD, near)
    attend(SIDE, 96)
    cps["far", 2].wait_recv()
    cps["far", 0].wait_recv()
    attend(FAR, 96)
    cps["far", 1] = send(dqp.at[rng(FAR)], dqr.at[rng(FAR)], S_FAR + 1, far)
    cps["fwd", 2].wait_recv()
    cps["fwd", 0].wait_recv()
    attend(NSIDE, 96)
    cps["fwd", 1] = send(dqp.at[rng(NSIDE)], dqn, S_FWD + 1, near)
    for name in ("cr", "cl"):
        cps[name, 2].wait_recv()
        cps[name, 0].wait_recv()
    attend(CORNER, 96)
    cps["cr", 1] = send(dqp.at[rng(CORNER, 48)], dqr.at[rng(CORNER, 48)], S_CR + 1, far_left)
    cps["cl", 1] = send(
        dqp.at[rng(CORNER + 48, 48)], dqr.at[rng(CORNER + 48, 48)], S_CL + 1, far_right
    )
    cps["fwd", 1].wait_recv()
    side_sum[...] = (dqp[SIDE : SIDE + 96, :].astype(F32) + dqn[...].astype(F32)).astype(BF)
    cps["right", 1] = send(side_sum.at[rng(0, 48)], dqr.at[rng(SIDE, 48)], S_RIGHT + 1, left)
    cps["left", 1] = send(
        side_sum.at[rng(48, 48)], dqr.at[rng(SIDE + 48, 48)], S_LEFT + 1, right
    )

    dk = gather(0, 0.125).astype(BF)
    dv = (gather(1, 1.0) * key_open).astype(BF)
    dmine[1] = dk
    dmine[2] = dv
    cps["dkv"] = send(dmine.at[pl.ds(1, 2)], dother.at[pl.ds(1, 2)], S_DKV, near)
    cps["hx"].wait_recv()
    cps["dkv"].wait_recv()

    def partial(m, t):
        total = dot(hp[core, t], dmine[m], ((0,), (0,)))
        return total + dot(hx[t], dother[m], ((0,), (0,)))

    for m in (1, 2):
        w = partial(m, 1)
        for i in range(nx):
            piece = w[96 * i : 96 * i + 96]
            dw[i, :, 384 * m : 384 * m + 384] = piece
            xs_kv[i, :, 384 * (m - 1) : 384 * m] = piece.astype(BF)
    for v, d in x_peers:
        cps["xkv", d] = send(xs_kv.at[v], xr_kv.at[d - 1], S_X + d - 1, x_dev(v))
    ihcg_ref[...] = (
        dot(dk, wk_ref[...], ((1,), (1,))) + dot(dv, wv_ref[...], ((1,), (1,)))
    ).astype(BF)
    leave(1, ihcg_ref, ihcg_out)
    dqa[...] = dqp[0:128, :].astype(F32)
    cps["near", 1].wait_recv()
    dqa[near_at, :] += dqr[NEAR : NEAR + 96, :].astype(F32)
    for name in ("far", "cr", "cl", "right", "left"):
        cps[name, 1].wait_recv()
    dqa[far_at, :] += dqr[FAR : FAR + 96, :].astype(F32)
    edges = dot(pack_ref[...], dqr[SIDE : SIDE + 96, :], ((0,), (0,)))
    edges = edges + dot(pack_ref[...], dqr[CORNER : CORNER + 96, :], ((0,), (0,)))
    dq = (dqa[...] + edges).astype(BF)
    dmine[0] = dq
    cps["dq"] = send(dmine.at[0], dother.at[0], S_DQ, near)
    heg_ref[...] = dot(dq, wq_ref[...], ((1,), (1,))).astype(BF)
    leave(0, heg_ref, heg_out)
    cps["dq"].wait_recv()
    w = partial(0, 0)
    for i in range(nx):
        piece = w[96 * i : 96 * i + 96]
        dw[i, :, 0:384] = piece
        xs_q[i] = piece.astype(BF)
    for v, d in x_peers:
        cps["xq", d] = send(xs_q.at[v], xr_q.at[d - 1], S_X + 3 + d - 1, x_dev(v))
    def to_y(dst, at, total):
        laid = dot(total.astype(BF), toy_ref[...]).astype(BF)
        for h in range(2):
            for l in range(4):
                dst[4 * h + l, :, 128 * at : 128 * at + 128] = laid[
                    48 * h : 48 * h + 48, 128 * l : 128 * l + 128
                ]

    for _, d in x_peers:
        cps["xkv", d].wait_recv()
    for m in (1, 2):
        total = dw[x, :, 384 * m : 384 * m + 384]
        for _, d in x_peers:
            total = total + xr_kv[d - 1, :, 384 * (m - 1) : 384 * m].astype(F32)
        to_y(ys_kv, m - 1, total)
    for v, d in y_peers:
        cps["ykv", d] = send(ys_kv.at[v], yr_kv.at[d - 1], S_YKV + d - 1, y_dev(v))
    for _, d in x_peers:
        cps["xq", d].wait_recv()
    total = dw[x, :, 0:384]
    for _, d in x_peers:
        total = total + xr_q[d - 1].astype(F32)
    to_y(ys_q, 0, total)
    for v, d in y_peers:
        cps["yq", d] = send(ys_q.at[v], yr_q.at[d - 1], S_YQ + d - 1, y_dev(v))
    total_kv = ys_kv[y].astype(F32)
    for _, d in y_peers:
        cps["ykv", d].wait_recv()
        total_kv = total_kv + yr_kv[d - 1].astype(F32)
    total_q = ys_q[y].astype(F32)
    for _, d in y_peers:
        cps["yq", d].wait_recv()
        total_q = total_q + yr_q[d - 1].astype(F32)
    total = jnp.concatenate([total_q, total_kv], axis=1)
    laid = dot(total.astype(BF), toz_ref[...]).astype(BF)
    for i in range(nz):
        zs[i] = laid[:, 128 * i : 128 * i + 128]
    for v, d in z_peers:
        cps["z", d] = send(zs.at[v], zr.at[d - 1], S_Z + d - 1, z_dev(v))
    total = zs[z].astype(F32)
    for _, d in z_peers:
        cps["z", d].wait_recv()
        total = total + zr[d - 1].astype(F32)
    total = total * (1.0 / math.sqrt(128.0 * rows * cols))
    turned = total.T
    for m in range(3):
        wg_ref[m] = turned[12 * m : 12 * m + 12, :]
    leave(2, wg_ref, wg_out)
    for cp in started:
        cp.wait_send()
    for cp in outs:
        cp.wait()


def write_out(a_in, b_in, c_in, a_out, b_out, c_out, a, b, c, sem):
    held = ((a_in, a, a_out), (b_in, b, b_out), (c_in, c, c_out))
    loads = [pltpu.make_async_copy(h[0], h[1], sem.at[0, i]) for i, h in enumerate(held)]
    stores = [pltpu.make_async_copy(h[1], h[2], sem.at[1, i]) for i, h in enumerate(held)]
    for cp in loads:
        cp.start()
    for load, store in zip(loads, stores):
        load.wait()
        store.start()
    for cp in stores:
        cp.wait()


def on_device(rows, cols, he, ihc, he_mask, ihc_mask, offsets, wq, wk, wv, grad_out):
    nx, nz = rows // 4, cols // 4
    consts = constants()
    args = (
        offsets,
        he.reshape(128, 768), ihc.reshape(128, 768),
        he_mask, ihc_mask,
        wq, wk, wv, grad_out.reshape(128, 384), *consts,
    )
    heg, ihcg, wg = pl.pallas_call(
        functools.partial(kernel, rows, cols),
        out_shape=(
            jax.ShapeDtypeStruct((128, 768), BF),
            jax.ShapeDtypeStruct((128, 768), BF),
            jax.ShapeDtypeStruct((3, 12, 48), F32),
        ),
        in_specs=[pl.BlockSpec(memory_space=pltpu.HBM)] * len(args),
        out_specs=[pl.BlockSpec(memory_space=pltpu.HBM)] * 3,
        scratch_shapes=[
            pltpu.VMEM((128, 768), BF),
            pltpu.VMEM((128, 768), BF),
            pltpu.VMEM((3, 12, 48), F32),
            pltpu.SemaphoreType.DMA((3,)),
        ]
        + [pltpu.VMEM(a.shape, a.dtype) for a in args]
        + [
            pltpu.SemaphoreType.DMA((len(args),)),
            pltpu.VMEM((ROWS, 768), BF),
            pltpu.VMEM((128, 768), BF),
            pltpu.VMEM((96, 768), BF),
            pltpu.VMEM((I_ALL, 16, 128), BF),
            pltpu.VMEM((ROWS, 128), BF),
            pltpu.VMEM((2, PAIRS, 256, 128), BF),
            pltpu.VMEM((2, PAIRS, 256, 128), F32),
            pltpu.VMEM((ROWS, 384), BF),
            pltpu.VMEM((ROWS, 384), BF),
            pltpu.VMEM((96, 384), BF),
            pltpu.VMEM((96, 384), BF),
            pltpu.VMEM((128, 384), F32),
            pltpu.VMEM((2, 2, 128, 384), BF),
            pltpu.VMEM((2, 128, 384), BF),
            pltpu.VMEM((3, 128, 384), BF),
            pltpu.VMEM((3, 128, 384), BF),
            pltpu.VMEM((nx, 96, 1152), F32),
            pltpu.VMEM((nx, 96, 384), BF),
            pltpu.VMEM((nx - 1, 96, 384), BF),
            pltpu.VMEM((nx, 96, 768), BF),
            pltpu.VMEM((nx - 1, 96, 768), BF),
            pltpu.VMEM((8, 48, 128), BF),
            pltpu.VMEM((7, 48, 128), BF),
            pltpu.VMEM((8, 48, 256), BF),
            pltpu.VMEM((7, 48, 256), BF),
            pltpu.VMEM((nz, 48, 128), BF),
            pltpu.VMEM((nz - 1, 48, 128), BF),
            pltpu.SemaphoreType.DMA((S_ALL,)),
            pltpu.SemaphoreType.DMA((S_ALL,)),
        ],
        compiler_params=pltpu.CompilerParams(
            collective_id=0, has_side_effects=True, vmem_limit_bytes=56 << 20
        ),
    )(*args)
    parts = (heg, ihcg, wg)
    heg, ihcg, wg = pl.pallas_call(
        write_out,
        out_shape=tuple(jax.ShapeDtypeStruct(a.shape, a.dtype) for a in parts),
        in_specs=[pl.BlockSpec(memory_space=pl.ANY)] * 3,
        out_specs=[pl.BlockSpec(memory_space=pltpu.HBM)] * 3,
        scratch_shapes=[pltpu.VMEM(a.shape, a.dtype) for a in parts]
        + [pltpu.SemaphoreType.DMA((2, 3))],
        compiler_params=pltpu.CompilerParams(vmem_limit_bytes=60 << 20),
    )(*parts)
    return heg.reshape(8, 16, 768), ihcg.reshape(8, 16, 768), jnp.swapaxes(wg, 1, 2)


def solution(mesh):
    placed = (
        P("row", "col", None), P("row", "col", None), P("row", "col"), P("row", "col"),
        P("row", "col", None), P(), P(), P(), P("row", "col", None),
    )
    return jax.shard_map(
        functools.partial(on_device, mesh.shape["row"], mesh.shape["col"]),
        mesh=mesh,
        in_specs=placed,
        out_specs=(P("row", "col", None), P("row", "col", None), P(None, "row", "col")),
        check_vma=False,
    )
```

```python
import functools
import math

import jax
import jax.numpy as jnp
import numpy as np
from jax import lax
from jax.experimental import pallas as pl
from jax.experimental.pallas import tpu as pltpu
from jax.sharding import PartitionSpec as P

MESH = pl.DeviceIdType.MESH
BF = jnp.bfloat16
F32 = jnp.float32
PAIRS = 3
OWN, NEAR, SIDE, NSIDE, FAR, CORNER, ROWS = 0, 128, 224, 320, 416, 512, 608
S_NEAR, S_FAR, S_RIGHT, S_LEFT, S_FWD, S_CR, S_CL = 0, 5, 10, 15, 20, 25, 30
S_HX, S_DKV, S_DQ, S_X, S_YKV, S_YQ, S_Z, S_ALL = 35, 36, 37, 38, 44, 51, 58, 65
GROUPS = (((0, 1), pl.ds(0, 512), pl.ds(0, 256)), ((2,), pl.ds(512, 256), pl.ds(256, 128)))
I_OWN, I_NEAR, I_SIDE, I_NSIDE, I_FAR, I_CORNER, I_ALL = 0, 1, 2, 4, 6, 7, 9


def constants():
    n = np.arange(48)
    pack = np.zeros((96, 128), np.float32)
    pack[n, (n // 6) * 16 + 10 + n % 6] = 1
    pack[48 + n, (n // 6) * 16 + n % 6] = 1
    perm = np.zeros((768, 768), np.float32)
    f = np.arange(768)
    slab, inner = f // 48, f % 48
    perm[f, (slab % 2) * 384 + (slab // 2) * 48 + inner] = 1
    to_y = np.zeros((384, 512), np.float32)
    lane = np.arange(384)
    c, j = lane // 12, lane % 12
    to_y[lane, (c % 4) * 128 + (c // 4) * 12 + j] = 1
    to_z = np.zeros((384, 1024), np.float32)
    for part in range(3):
        k = np.arange(96)
        to_z[part * 128 + k, (k // 12) * 128 + part * 12 + k % 12] = 1
    spread = np.zeros((128, 256), np.float32)
    spread[0, :128] = 1
    spread[64, 128:] = 1
    place = np.zeros((2, ROWS, 128), np.float32)
    for core in range(2):
        near0, far0 = (8, -6) if core == 0 else (-6, 8)
        own = np.arange(128)
        row, col = np.zeros(ROWS), np.zeros(ROWS)
        row[:128], col[:128] = own // 16, own % 16
        w = np.arange(96)
        row[NEAR : NEAR + 96], col[NEAR : NEAR + 96] = near0 + w // 16, w % 16
        row[FAR : FAR + 96], col[FAR : FAR + 96] = far0 + w // 16, w % 16
        s = w % 48
        scol = np.where(w < 48, -6 + s % 6, 16 + s % 6)
        row[SIDE : SIDE + 96], col[SIDE : SIDE + 96] = s // 6, scol
        row[NSIDE : NSIDE + 96] = (8 if core == 0 else -8) + s // 6
        col[NSIDE : NSIDE + 96] = scol
        row[CORNER : CORNER + 96] = (-8 if core == 0 else 8) + s // 6
        col[CORNER : CORNER + 96] = scol
        place[core, :, 0] = row
        place[core, :, 64] = col
    return [jnp.asarray(a, BF) for a in (pack, perm, to_y, to_z, spread, place)]


def dot(a, b, dims=((1,), (0,))):
    return lax.dot_general(a, b, (dims, ((), ())), preferred_element_type=F32)


def kernel(
    rows, cols,
    off_in, he_in, ihc_in, hm_in, im_in, wq_in, wk_in, wv_in, g_in,
    pack_in, perm_in, toy_in, toz_in, spread_in, place_in,
    heg_out, ihcg_out, wg_out,
    heg_ref, ihcg_ref, wg_ref, out_sem,
    off_ref, he_ref, ihc_ref, hm_ref, im_ref, wq_ref, wk_ref, wv_ref, g_ref,
    pack_ref, perm_ref, toy_ref, toz_ref, spread_ref, place_ref, in_sem,
    qg, kv, pq, info, place, bd, acc, closed, dqp, dqr, dqn, side_sum, dqa, hp, hx, dmine, dother, dw,
    xs_q, xr_q, xs_kv, xr_kv, ys_q, yr_q, ys_kv, yr_kv, zs, zr, send_sem, recv_sem,
):
    r, c = lax.axis_index("row"), lax.axis_index("col")
    x, yh, core = r // 4, lax.rem(r // 2, 2), lax.rem(r, 2)
    z, yl = c // 4, lax.rem(c, 4)
    y = yh * 4 + yl
    nx, nz = rows // 4, cols // 4
    near = (r + 1 - 2 * core, c)
    far = (lax.rem(r + 2 * core - 1 + rows, rows), c)
    right = (r, lax.rem(c + 1, cols))
    left = (r, lax.rem(c + cols - 1, cols))
    far_right, far_left = (far[0], right[1]), (far[0], left[1])
    x_peers = [(lax.rem(x + d, nx), d) for d in range(1, nx)]
    y_peers = [(lax.rem(y + d, 8), d) for d in range(1, 8)]
    z_peers = [(lax.rem(z + d, nz), d) for d in range(1, nz)]

    def x_dev(v):
        return (v * 4 + yh * 2 + core, c)

    def y_dev(v):
        return (x * 4 + (v // 4) * 2 + core, z * 4 + lax.rem(v, 4))

    def z_dev(v):
        return (r, v * 4 + yl)

    partners = [near, far, right, left, far_right, far_left]
    partners += [x_dev(v) for v, _ in x_peers]
    partners += [y_dev(v) for v, _ in y_peers]
    partners += [z_dev(v) for v, _ in z_peers]
    barrier = pltpu.get_barrier_semaphore()
    for dev in partners:
        pl.semaphore_signal(barrier, inc=1, device_id=dev, device_id_type=MESH)

    loads = {}
    order = (
        (he_in, he_ref), (wq_in, wq_ref), (g_in, g_ref), (hm_in, hm_ref), (off_in, off_ref),
        (pack_in, pack_ref), (ihc_in, ihc_ref), (wk_in, wk_ref), (wv_in, wv_ref),
        (im_in, im_ref), (perm_in, perm_ref), (place_in, place_ref), (spread_in, spread_ref),
        (toy_in, toy_ref), (toz_in, toz_ref),
    )
    for i, (src, dst) in enumerate(order):
        loads[i] = pltpu.make_async_copy(src, dst, in_sem.at[i])
    for i in range(6):
        loads[i].start()

    def ready(*which):
        for i in which:
            loads[i].wait()

    outs = []

    def leave(i, src, dst):
        cp = pltpu.make_async_copy(src, dst, out_sem.at[i])
        cp.start()
        outs.append(cp)

    started = []

    def send(src, dst, sem, dev):
        cp = pltpu.make_async_remote_copy(
            src_ref=src, dst_ref=dst, send_sem=send_sem.at[sem], recv_sem=recv_sem.at[sem],
            device_id=dev, device_id_type=MESH,
        )
        cp.start()
        started.append(cp)
        return cp

    tile = lax.broadcasted_iota(jnp.int32, (128, 128), 0)
    lane = lax.broadcasted_iota(jnp.int32, (128, 128), 1)

    def column(mask):
        mine = (tile[:, 0:8] // 16 == lane[:, 0:8]).astype(F32)
        spread = dot(mine, mask.astype(F32))
        here = lax.rem(tile[:, 0:16], 16) == lane[:, 0:16]
        return jnp.sum(jnp.where(here, spread, 0.0), axis=1, keepdims=True)

    ready(0, 1)
    for i in range(6, len(order)):
        loads[i].start()
    q = dot(he_ref[...], wq_ref[...]).astype(BF)
    ready(2, 3, 4, 5)
    g = (g_ref[...].astype(F32) * column(hm_ref[...])).astype(BF)
    for h in range(PAIRS):
        qg[0:128, 256 * h : 256 * h + 128] = q[:, 128 * h : 128 * h + 128]
        qg[0:128, 256 * h + 128 : 256 * h + 256] = g[:, 128 * h : 128 * h + 128]
    off = off_ref[0].astype(F32)
    a0, b0, a1, b1 = off[0:1, 0:1], off[0:1, 1:2], off[1:2, 0:1], off[1:2, 1:2]
    block = jnp.where(lane < 64, jnp.where(tile == 0, a0, a1), jnp.where(tile == 0, b0, b1))
    info[I_OWN] = block[0:16].astype(BF)
    pq[...] = dot(pack_ref[...], qg[0:128, :]).astype(BF)
    pl.semaphore_wait(barrier, len(partners))

    near_at = pl.ds(pl.multiple_of(32 * (1 - core), 32), 96)
    far_at = pl.ds(pl.multiple_of(32 * core, 32), 96)

    def rng(start, size=96):
        return pl.ds(start, size)

    cps = {}
    own_info = info.at[I_OWN]
    cps["far", 2] = send(own_info, info.at[I_FAR], S_FAR + 2, far)
    cps["near", 2] = send(own_info, info.at[I_NEAR], S_NEAR + 2, near)
    cps["right", 2] = send(own_info, info.at[I_SIDE], S_RIGHT + 2, right)
    cps["left", 2] = send(own_info, info.at[I_SIDE + 1], S_LEFT + 2, left)
    cps["cr", 2] = send(own_info, info.at[I_CORNER], S_CR + 2, far_right)
    cps["cl", 2] = send(own_info, info.at[I_CORNER + 1], S_CL + 2, far_left)
    for t, (_, lanes, _) in enumerate(GROUPS):
        to_right, to_left = pq.at[rng(0, 48), lanes], pq.at[rng(48, 48), lanes]
        cps["far", t] = send(qg.at[far_at, lanes], qg.at[rng(FAR), lanes], S_FAR + t, far)
        cps["cr", t] = send(to_right, qg.at[rng(CORNER, 48), lanes], S_CR + t, far_right)
        cps["cl", t] = send(to_left, qg.at[rng(CORNER + 48, 48), lanes], S_CL + t, far_left)
        cps["right", t] = send(to_right, qg.at[rng(SIDE, 48), lanes], S_RIGHT + t, right)
        cps["left", t] = send(to_left, qg.at[rng(SIDE + 48, 48), lanes], S_LEFT + t, left)
        cps["near", t] = send(qg.at[near_at, lanes], qg.at[rng(NEAR), lanes], S_NEAR + t, near)

    ready(6, 7, 8, 9)
    ihc = ihc_ref[...]
    key_open = column(im_ref[...])
    kv[0:128, 0:384] = (dot(ihc, wk_ref[...]) * key_open).astype(BF)
    kv[0:128, 384:768] = (dot(ihc, wv_ref[...]) * key_open).astype(BF)

    ready(*range(10, 15))
    for t, ref in enumerate((he_ref, ihc_ref)):
        ordered = dot(ref[...], perm_ref[...]).astype(BF)
        hp[0, t] = ordered[:, 0:384]
        hp[1, t] = ordered[:, 384:768]
    cps["hx"] = send(hp.at[1 - core], hx, S_HX, near)

    place[...] = place_ref[core]
    row_bad = jnp.where(core == 0, (r == 0).astype(F32), (r == rows - 1).astype(F32)) * 1024.0
    left_bad = (c == 0).astype(F32) * 1024.0
    right_bad = (c == cols - 1).astype(F32) * 1024.0

    def shift(start, size, amount):
        place[start : start + size, :] = (
            place[start : start + size, :].astype(F32) + amount
        ).astype(BF)

    for base in (SIDE, NSIDE):
        shift(base, 48, left_bad)
        shift(base + 48, 48, right_bad)
    shift(FAR, 96, row_bad)
    shift(CORNER, 48, left_bad + row_bad)
    shift(CORNER + 48, 48, right_bad + row_bad)

    low = lane < 64
    zero = jnp.zeros((128, 128), BF)
    for i, base in enumerate((0, 384)):
        for h in range(PAIRS):
            part = kv[0:128, base + 128 * h : base + 128 * h + 128]
            bd[i, h, 0:128, :] = jnp.where(low, part, zero)
            bd[i, h, 128:256, :] = jnp.where(low, zero, part)
    acc[...] = jnp.zeros(acc.shape, F32)

    vec = lax.broadcasted_iota(jnp.int32, (1, 128), 1)
    lane_row = (vec // 16).astype(F32)
    lane_col = lax.rem(vec, 16).astype(F32)
    shift_open = math.log(25.0)

    slots = {NEAR: I_NEAR, SIDE: I_SIDE, NSIDE: I_NSIDE, FAR: I_FAR, CORNER: I_CORNER}

    def shifts(start, size):
        slot = slots.get(start, I_OWN)
        if start in (SIDE, NSIDE, CORNER):
            chosen = jnp.where(tile[0:size, 0:32] < 48, 1, 16) == lane[0:size, 0:32]
            table = jnp.concatenate([info[slot], info[slot + 1]], axis=0)
        else:
            chosen = lax.rem(tile[0:size, 0:16], 16) // 8 == lane[0:size, 0:16]
            table = info[slot]
        return dot(chosen.astype(F32).astype(BF), table).astype(BF)

    def attend(t, start, size):
        if t == 0:
            where_at = place[start : start + size, :] + shifts(start, size)
            at = dot(where_at, spread_ref[...])
            gap = jnp.maximum(
                jnp.abs(at[:, 0:128] - lane_row), jnp.abs(at[:, 128:256] - lane_col)
            )
            bias = jnp.where(gap <= 2.5, shift_open, 1e9)
            closed[start : start + size, :] = bias
        else:
            bias = closed[start : start + size, :]
        bias = jnp.concatenate([bias, bias], axis=1)
        for h in GROUPS[t][0]:
            one = qg[start : start + size, 256 * h : 256 * h + 128]
            two = qg[start : start + size, 256 * h + 128 : 256 * h + 256]
            score = dot(one, bd[0, h], ((1,), (1,)))
            dweight = dot(two, bd[1, h], ((1,), (1,)))
            e = jnp.exp(jnp.minimum(bias - score * 0.125, 88.0))
            sig = 1.0 / (1.0 + e)
            dscore = (dweight * (sig * (1.0 - sig))).astype(BF)
            acc[0, h] += dot(dscore, one, ((0,), (0,)))
            acc[1, h] += dot(sig.astype(BF), two, ((0,), (0,)))
            back = dot(dscore, bd[0, h]) * 0.125
            dqp[start : start + size, 128 * h : 128 * h + 128] = back.astype(BF)

    def gather(i, scale):
        parts = [jnp.where(low, acc[i, h, 0:128], acc[i, h, 128:256]) * scale for h in range(PAIRS)]
        return jnp.concatenate(parts, axis=1)

    def arrived(t, *names):
        for name in names:
            if t == 0:
                cps[name, 2].wait_recv()
            cps[name, t].wait_recv()

    attend(0, OWN, 128)
    attend(1, OWN, 128)
    for t, (_, lanes, part) in enumerate(GROUPS):
        arrived(t, "near")
        attend(t, NEAR, 96)
        near_rows = (rng(NEAR), part)
        cps["near", 3 + t] = send(
            dqp.at[near_rows], dqr.at[near_rows], S_NEAR + 3 + t, near
        )
        arrived(t, "right", "left")
        if t == 0:
            cps["fwd", 2] = send(
                info.at[pl.ds(I_SIDE, 2)], info.at[pl.ds(I_NSIDE, 2)], S_FWD + 2, near
            )
        cps["fwd", t] = send(
            qg.at[rng(SIDE), lanes], qg.at[rng(NSIDE), lanes], S_FWD + t, near
        )
        attend(t, SIDE, 96)
        arrived(t, "far")
        attend(t, FAR, 96)
        far_rows = (rng(FAR), part)
        cps["far", 3 + t] = send(dqp.at[far_rows], dqr.at[far_rows], S_FAR + 3 + t, far)
        arrived(t, "fwd")
        attend(t, NSIDE, 96)
        cps["fwd", 3 + t] = send(
            dqp.at[rng(NSIDE), part], dqn.at[rng(0), part], S_FWD + 3 + t, near
        )
        arrived(t, "cr", "cl")
        attend(t, CORNER, 96)
        one, two = (rng(CORNER, 48), part), (rng(CORNER + 48, 48), part)
        cps["cr", 3 + t] = send(dqp.at[one], dqr.at[one], S_CR + 3 + t, far_left)
        cps["cl", 3 + t] = send(dqp.at[two], dqr.at[two], S_CL + 3 + t, far_right)
        cps["fwd", 3 + t].wait_recv()
        side_sum[:, part] = (
            dqp[SIDE : SIDE + 96, part].astype(F32) + dqn[:, part].astype(F32)
        ).astype(BF)
        cps["right", 3 + t] = send(
            side_sum.at[rng(0, 48), part], dqr.at[rng(SIDE, 48), part], S_RIGHT + 3 + t, left
        )
        cps["left", 3 + t] = send(
            side_sum.at[rng(48, 48), part], dqr.at[rng(SIDE + 48, 48), part],
            S_LEFT + 3 + t, right,
        )

    dk = gather(0, 0.125).astype(BF)
    dv = (gather(1, 1.0) * key_open).astype(BF)
    dmine[1] = dk
    dmine[2] = dv
    cps["dkv"] = send(dmine.at[pl.ds(1, 2)], dother.at[pl.ds(1, 2)], S_DKV, near)
    cps["hx"].wait_recv()
    cps["dkv"].wait_recv()

    def partial(m, t):
        total = dot(hp[core, t], dmine[m], ((0,), (0,)))
        return total + dot(hx[t], dother[m], ((0,), (0,)))

    for m in (1, 2):
        w = partial(m, 1)
        for i in range(nx):
            piece = w[96 * i : 96 * i + 96]
            dw[i, :, 384 * m : 384 * m + 384] = piece
            xs_kv[i, :, 384 * (m - 1) : 384 * m] = piece.astype(BF)
    for v, d in x_peers:
        cps["xkv", d] = send(xs_kv.at[v], xr_kv.at[d - 1], S_X + d - 1, x_dev(v))
    ihcg_ref[...] = (
        dot(dk, wk_ref[...], ((1,), (1,))) + dot(dv, wv_ref[...], ((1,), (1,)))
    ).astype(BF)
    leave(1, ihcg_ref, ihcg_out)
    dqa[...] = dqp[0:128, :].astype(F32)
    for t in range(2):
        cps["near", 3 + t].wait_recv()
    dqa[near_at, :] += dqr[NEAR : NEAR + 96, :].astype(F32)
    for name in ("far", "cr", "cl", "right", "left"):
        for t in range(2):
            cps[name, 3 + t].wait_recv()
    dqa[far_at, :] += dqr[FAR : FAR + 96, :].astype(F32)
    edges = dot(pack_ref[...], dqr[SIDE : SIDE + 96, :], ((0,), (0,)))
    edges = edges + dot(pack_ref[...], dqr[CORNER : CORNER + 96, :], ((0,), (0,)))
    dq = (dqa[...] + edges).astype(BF)
    dmine[0] = dq
    cps["dq"] = send(dmine.at[0], dother.at[0], S_DQ, near)
    heg_ref[...] = dot(dq, wq_ref[...], ((1,), (1,))).astype(BF)
    leave(0, heg_ref, heg_out)
    cps["dq"].wait_recv()
    w = partial(0, 0)
    for i in range(nx):
        piece = w[96 * i : 96 * i + 96]
        dw[i, :, 0:384] = piece
        xs_q[i] = piece.astype(BF)
    for v, d in x_peers:
        cps["xq", d] = send(xs_q.at[v], xr_q.at[d - 1], S_X + 3 + d - 1, x_dev(v))
    def to_y(dst, at, total):
        laid = dot(total.astype(BF), toy_ref[...]).astype(BF)
        for h in range(2):
            for l in range(4):
                dst[4 * h + l, :, 128 * at : 128 * at + 128] = laid[
                    48 * h : 48 * h + 48, 128 * l : 128 * l + 128
                ]

    for _, d in x_peers:
        cps["xkv", d].wait_recv()
    for m in (1, 2):
        total = dw[x, :, 384 * m : 384 * m + 384]
        for _, d in x_peers:
            total = total + xr_kv[d - 1, :, 384 * (m - 1) : 384 * m].astype(F32)
        to_y(ys_kv, m - 1, total)
    for v, d in y_peers:
        cps["ykv", d] = send(ys_kv.at[v], yr_kv.at[d - 1], S_YKV + d - 1, y_dev(v))
    for _, d in x_peers:
        cps["xq", d].wait_recv()
    total = dw[x, :, 0:384]
    for _, d in x_peers:
        total = total + xr_q[d - 1].astype(F32)
    to_y(ys_q, 0, total)
    for v, d in y_peers:
        cps["yq", d] = send(ys_q.at[v], yr_q.at[d - 1], S_YQ + d - 1, y_dev(v))
    total_kv = ys_kv[y].astype(F32)
    for _, d in y_peers:
        cps["ykv", d].wait_recv()
        total_kv = total_kv + yr_kv[d - 1].astype(F32)
    total_q = ys_q[y].astype(F32)
    for _, d in y_peers:
        cps["yq", d].wait_recv()
        total_q = total_q + yr_q[d - 1].astype(F32)
    total = jnp.concatenate([total_q, total_kv], axis=1)
    laid = dot(total.astype(BF), toz_ref[...]).astype(BF)
    for i in range(nz):
        zs[i] = laid[:, 128 * i : 128 * i + 128]
    for v, d in z_peers:
        cps["z", d] = send(zs.at[v], zr.at[d - 1], S_Z + d - 1, z_dev(v))
    total = zs[z].astype(F32)
    for _, d in z_peers:
        cps["z", d].wait_recv()
        total = total + zr[d - 1].astype(F32)
    total = total * (1.0 / math.sqrt(128.0 * rows * cols))
    turned = total.T
    for m in range(3):
        wg_ref[m] = turned[12 * m : 12 * m + 12, :]
    leave(2, wg_ref, wg_out)
    for cp in started:
        cp.wait_send()
    for cp in outs:
        cp.wait()


def write_out(a_in, b_in, c_in, a_out, b_out, c_out, a, b, c, sem):
    held = ((a_in, a, a_out), (b_in, b, b_out), (c_in, c, c_out))
    loads = [pltpu.make_async_copy(h[0], h[1], sem.at[0, i]) for i, h in enumerate(held)]
    stores = [pltpu.make_async_copy(h[1], h[2], sem.at[1, i]) for i, h in enumerate(held)]
    for cp in loads:
        cp.start()
    for load, store in zip(loads, stores):
        load.wait()
        store.start()
    for cp in stores:
        cp.wait()


def on_device(rows, cols, he, ihc, he_mask, ihc_mask, offsets, wq, wk, wv, grad_out):
    nx, nz = rows // 4, cols // 4
    consts = constants()
    args = (
        offsets,
        he.reshape(128, 768), ihc.reshape(128, 768),
        he_mask, ihc_mask,
        wq, wk, wv, grad_out.reshape(128, 384), *consts,
    )
    heg, ihcg, wg = pl.pallas_call(
        functools.partial(kernel, rows, cols),
        out_shape=(
            jax.ShapeDtypeStruct((128, 768), BF),
            jax.ShapeDtypeStruct((128, 768), BF),
            jax.ShapeDtypeStruct((3, 12, 48), F32),
        ),
        in_specs=[pl.BlockSpec(memory_space=pltpu.HBM)] * len(args),
        out_specs=[pl.BlockSpec(memory_space=pltpu.HBM)] * 3,
        scratch_shapes=[
            pltpu.VMEM((128, 768), BF),
            pltpu.VMEM((128, 768), BF),
            pltpu.VMEM((3, 12, 48), F32),
            pltpu.SemaphoreType.DMA((3,)),
        ]
        + [pltpu.VMEM(a.shape, a.dtype) for a in args]
        + [
            pltpu.SemaphoreType.DMA((len(args),)),
            pltpu.VMEM((ROWS, 768), BF),
            pltpu.VMEM((128, 768), BF),
            pltpu.VMEM((96, 768), BF),
            pltpu.VMEM((I_ALL, 16, 128), BF),
            pltpu.VMEM((ROWS, 128), BF),
            pltpu.VMEM((2, PAIRS, 256, 128), BF),
            pltpu.VMEM((2, PAIRS, 256, 128), F32),
            pltpu.VMEM((ROWS, 128), F32),
            pltpu.VMEM((ROWS, 384), BF),
            pltpu.VMEM((ROWS, 384), BF),
            pltpu.VMEM((96, 384), BF),
            pltpu.VMEM((96, 384), BF),
            pltpu.VMEM((128, 384), F32),
            pltpu.VMEM((2, 2, 128, 384), BF),
            pltpu.VMEM((2, 128, 384), BF),
            pltpu.VMEM((3, 128, 384), BF),
            pltpu.VMEM((3, 128, 384), BF),
            pltpu.VMEM((nx, 96, 1152), F32),
            pltpu.VMEM((nx, 96, 384), BF),
            pltpu.VMEM((nx - 1, 96, 384), BF),
            pltpu.VMEM((nx, 96, 768), BF),
            pltpu.VMEM((nx - 1, 96, 768), BF),
            pltpu.VMEM((8, 48, 128), BF),
            pltpu.VMEM((7, 48, 128), BF),
            pltpu.VMEM((8, 48, 256), BF),
            pltpu.VMEM((7, 48, 256), BF),
            pltpu.VMEM((nz, 48, 128), BF),
            pltpu.VMEM((nz - 1, 48, 128), BF),
            pltpu.SemaphoreType.DMA((S_ALL,)),
            pltpu.SemaphoreType.DMA((S_ALL,)),
        ],
        compiler_params=pltpu.CompilerParams(
            collective_id=0, has_side_effects=True, vmem_limit_bytes=56 << 20
        ),
    )(*args)
    parts = (heg, ihcg, wg)
    heg, ihcg, wg = pl.pallas_call(
        write_out,
        out_shape=tuple(jax.ShapeDtypeStruct(a.shape, a.dtype) for a in parts),
        in_specs=[pl.BlockSpec(memory_space=pl.ANY)] * 3,
        out_specs=[pl.BlockSpec(memory_space=pltpu.HBM)] * 3,
        scratch_shapes=[pltpu.VMEM(a.shape, a.dtype) for a in parts]
        + [pltpu.SemaphoreType.DMA((2, 3))],
        compiler_params=pltpu.CompilerParams(vmem_limit_bytes=60 << 20),
    )(*parts)
    return heg.reshape(8, 16, 768), ihcg.reshape(8, 16, 768), jnp.swapaxes(wg, 1, 2)


def solution(mesh):
    placed = (
        P("row", "col", None), P("row", "col", None), P("row", "col"), P("row", "col"),
        P("row", "col", None), P(), P(), P(), P("row", "col", None),
    )
    return jax.shard_map(
        functools.partial(on_device, mesh.shape["row"], mesh.shape["col"]),
        mesh=mesh,
        in_specs=placed,
        out_specs=(P("row", "col", None), P("row", "col", None), P(None, "row", "col")),
        check_vma=False,
    )
```

```python
import functools
import math

import jax
import jax.numpy as jnp
import numpy as np
from jax import lax
from jax.experimental import pallas as pl
from jax.experimental.pallas import tpu as pltpu
from jax.sharding import PartitionSpec as P

MESH = pl.DeviceIdType.MESH
BF = jnp.bfloat16
F32 = jnp.float32
PAIRS = 3
OWN, NEAR, SIDE, NSIDE, FAR, CORNER, ROWS = 0, 128, 224, 320, 416, 512, 608
S_NEAR, S_FAR, S_RIGHT, S_LEFT, S_FWD, S_CR, S_CL = 0, 5, 10, 15, 20, 25, 30
S_HX, S_DKV, S_DQ, S_X, S_YKV, S_YQ, S_Z, S_ALL = 35, 36, 37, 38, 47, 54, 61, 68
GROUPS = (((0, 1), pl.ds(0, 512), pl.ds(0, 256)), ((2,), pl.ds(512, 256), pl.ds(256, 128)))
I_OWN, I_NEAR, I_SIDE, I_NSIDE, I_FAR, I_CORNER, I_ALL = 0, 1, 2, 4, 6, 7, 9


def constants():
    n = np.arange(48)
    pack = np.zeros((96, 128), np.float32)
    pack[n, (n // 6) * 16 + 10 + n % 6] = 1
    pack[48 + n, (n // 6) * 16 + n % 6] = 1
    perm = np.zeros((768, 768), np.float32)
    f = np.arange(768)
    slab, inner = f // 48, f % 48
    perm[f, (slab % 2) * 384 + (slab // 2) * 48 + inner] = 1
    to_y = np.zeros((384, 512), np.float32)
    lane = np.arange(384)
    c, j = lane // 12, lane % 12
    to_y[lane, (c % 4) * 128 + (c // 4) * 12 + j] = 1
    to_z = np.zeros((384, 1024), np.float32)
    for part in range(3):
        k = np.arange(96)
        to_z[part * 128 + k, (k // 12) * 128 + part * 12 + k % 12] = 1
    spread = np.zeros((128, 256), np.float32)
    spread[0, :128] = 1
    spread[64, 128:] = 1
    place = np.zeros((2, ROWS, 128), np.float32)
    for core in range(2):
        near0, far0 = (8, -6) if core == 0 else (-6, 8)
        own = np.arange(128)
        row, col = np.zeros(ROWS), np.zeros(ROWS)
        row[:128], col[:128] = own // 16, own % 16
        w = np.arange(96)
        row[NEAR : NEAR + 96], col[NEAR : NEAR + 96] = near0 + w // 16, w % 16
        row[FAR : FAR + 96], col[FAR : FAR + 96] = far0 + w // 16, w % 16
        s = w % 48
        scol = np.where(w < 48, -6 + s % 6, 16 + s % 6)
        row[SIDE : SIDE + 96], col[SIDE : SIDE + 96] = s // 6, scol
        row[NSIDE : NSIDE + 96] = (8 if core == 0 else -8) + s // 6
        col[NSIDE : NSIDE + 96] = scol
        row[CORNER : CORNER + 96] = (-8 if core == 0 else 8) + s // 6
        col[CORNER : CORNER + 96] = scol
        place[core, :, 0] = row
        place[core, :, 64] = col
    return [jnp.asarray(a, BF) for a in (pack, perm, to_y, to_z, spread, place)]


def dot(a, b, dims=((1,), (0,))):
    return lax.dot_general(a, b, (dims, ((), ())), preferred_element_type=F32)


def kernel(
    rows, cols,
    off_in, he_in, ihc_in, hm_in, im_in, wq_in, wk_in, wv_in, g_in,
    pack_in, perm_in, toy_in, toz_in, spread_in, place_in,
    heg_out, ihcg_out, wg_out,
    heg_ref, ihcg_ref, wg_ref, out_sem,
    off_ref, he_ref, ihc_ref, hm_ref, im_ref, wq_ref, wk_ref, wv_ref, g_ref,
    pack_ref, perm_ref, toy_ref, toz_ref, spread_ref, place_ref, in_sem,
    qg, kv, pq, info, place, bd, acc, closed, dqp, dqr, dqn, side_sum, dqa, hp, hx, dmine, dother, dw,
    xs_q, xr_q, xs_kv, xr_kv, ys_q, yr_q, ys_kv, yr_kv, zs, zr, send_sem, recv_sem,
):
    r, c = lax.axis_index("row"), lax.axis_index("col")
    x, yh, core = r // 4, lax.rem(r // 2, 2), lax.rem(r, 2)
    z, yl = c // 4, lax.rem(c, 4)
    y = yh * 4 + yl
    nx, nz = rows // 4, cols // 4
    near = (r + 1 - 2 * core, c)
    far = (lax.rem(r + 2 * core - 1 + rows, rows), c)
    right = (r, lax.rem(c + 1, cols))
    left = (r, lax.rem(c + cols - 1, cols))
    far_right, far_left = (far[0], right[1]), (far[0], left[1])
    x_peers = [(lax.rem(x + d, nx), d) for d in range(1, nx)]
    y_peers = [(lax.rem(y + d, 8), d) for d in range(1, 8)]
    z_peers = [(lax.rem(z + d, nz), d) for d in range(1, nz)]

    def x_dev(v):
        return (v * 4 + yh * 2 + core, c)

    def y_dev(v):
        return (x * 4 + (v // 4) * 2 + core, z * 4 + lax.rem(v, 4))

    def z_dev(v):
        return (r, v * 4 + yl)

    partners = [near, far, right, left, far_right, far_left]
    partners += [x_dev(v) for v, _ in x_peers]
    partners += [y_dev(v) for v, _ in y_peers]
    partners += [z_dev(v) for v, _ in z_peers]
    barrier = pltpu.get_barrier_semaphore()
    for dev in partners:
        pl.semaphore_signal(barrier, inc=1, device_id=dev, device_id_type=MESH)

    loads = {}
    order = (
        (he_in, he_ref), (wq_in, wq_ref), (g_in, g_ref), (hm_in, hm_ref), (off_in, off_ref),
        (pack_in, pack_ref), (ihc_in, ihc_ref), (wk_in, wk_ref), (wv_in, wv_ref),
        (im_in, im_ref), (perm_in, perm_ref), (place_in, place_ref), (spread_in, spread_ref),
        (toy_in, toy_ref), (toz_in, toz_ref),
    )
    for i, (src, dst) in enumerate(order):
        loads[i] = pltpu.make_async_copy(src, dst, in_sem.at[i])
    for i in range(6):
        loads[i].start()

    def ready(*which):
        for i in which:
            loads[i].wait()

    outs = []

    def leave(i, src, dst):
        cp = pltpu.make_async_copy(src, dst, out_sem.at[i])
        cp.start()
        outs.append(cp)

    started = []

    def send(src, dst, sem, dev):
        cp = pltpu.make_async_remote_copy(
            src_ref=src, dst_ref=dst, send_sem=send_sem.at[sem], recv_sem=recv_sem.at[sem],
            device_id=dev, device_id_type=MESH,
        )
        cp.start()
        started.append(cp)
        return cp

    tile = lax.broadcasted_iota(jnp.int32, (128, 128), 0)
    lane = lax.broadcasted_iota(jnp.int32, (128, 128), 1)

    def column(mask):
        mine = (tile[:, 0:8] // 16 == lane[:, 0:8]).astype(F32)
        spread = dot(mine, mask.astype(F32))
        here = lax.rem(tile[:, 0:16], 16) == lane[:, 0:16]
        return jnp.sum(jnp.where(here, spread, 0.0), axis=1, keepdims=True)

    ready(0, 1)
    q = dot(he_ref[...], wq_ref[...]).astype(BF)
    ready(2, 3, 4, 5)
    g = (g_ref[...].astype(F32) * column(hm_ref[...])).astype(BF)
    for h in range(PAIRS):
        qg[0:128, 256 * h : 256 * h + 128] = q[:, 128 * h : 128 * h + 128]
        qg[0:128, 256 * h + 128 : 256 * h + 256] = g[:, 128 * h : 128 * h + 128]
    off = off_ref[0].astype(F32)
    a0, b0, a1, b1 = off[0:1, 0:1], off[0:1, 1:2], off[1:2, 0:1], off[1:2, 1:2]
    block = jnp.where(lane < 64, jnp.where(tile == 0, a0, a1), jnp.where(tile == 0, b0, b1))
    info[I_OWN] = block[0:16].astype(BF)
    pq[...] = dot(pack_ref[...], qg[0:128, :]).astype(BF)
    for i in range(6, len(order)):
        loads[i].start()
    pl.semaphore_wait(barrier, len(partners))

    near_at = pl.ds(pl.multiple_of(32 * (1 - core), 32), 96)
    far_at = pl.ds(pl.multiple_of(32 * core, 32), 96)

    def rng(start, size=96):
        return pl.ds(start, size)

    cps = {}
    own_info = info.at[I_OWN]
    cps["far", 2] = send(own_info, info.at[I_FAR], S_FAR + 2, far)
    cps["near", 2] = send(own_info, info.at[I_NEAR], S_NEAR + 2, near)
    cps["right", 2] = send(own_info, info.at[I_SIDE], S_RIGHT + 2, right)
    cps["left", 2] = send(own_info, info.at[I_SIDE + 1], S_LEFT + 2, left)
    cps["cr", 2] = send(own_info, info.at[I_CORNER], S_CR + 2, far_right)
    cps["cl", 2] = send(own_info, info.at[I_CORNER + 1], S_CL + 2, far_left)
    for t, (_, lanes, _) in enumerate(GROUPS):
        to_right, to_left = pq.at[rng(0, 48), lanes], pq.at[rng(48, 48), lanes]
        cps["far", t] = send(qg.at[far_at, lanes], qg.at[rng(FAR), lanes], S_FAR + t, far)
        cps["cr", t] = send(to_right, qg.at[rng(CORNER, 48), lanes], S_CR + t, far_right)
        cps["cl", t] = send(to_left, qg.at[rng(CORNER + 48, 48), lanes], S_CL + t, far_left)
        cps["right", t] = send(to_right, qg.at[rng(SIDE, 48), lanes], S_RIGHT + t, right)
        cps["left", t] = send(to_left, qg.at[rng(SIDE + 48, 48), lanes], S_LEFT + t, left)
        cps["near", t] = send(qg.at[near_at, lanes], qg.at[rng(NEAR), lanes], S_NEAR + t, near)

    ready(6, 7, 8, 9)
    ihc = ihc_ref[...]
    key_open = column(im_ref[...])
    kv[0:128, 0:384] = (dot(ihc, wk_ref[...]) * key_open).astype(BF)
    kv[0:128, 384:768] = (dot(ihc, wv_ref[...]) * key_open).astype(BF)

    ready(*range(10, 15))
    for t, ref in enumerate((he_ref, ihc_ref)):
        ordered = dot(ref[...], perm_ref[...]).astype(BF)
        hp[0, t] = ordered[:, 0:384]
        hp[1, t] = ordered[:, 384:768]
    cps["hx"] = send(hp.at[1 - core], hx, S_HX, near)

    place[...] = place_ref[core]
    row_bad = jnp.where(core == 0, (r == 0).astype(F32), (r == rows - 1).astype(F32)) * 1024.0
    left_bad = (c == 0).astype(F32) * 1024.0
    right_bad = (c == cols - 1).astype(F32) * 1024.0

    def shift(start, size, amount):
        place[start : start + size, :] = (
            place[start : start + size, :].astype(F32) + amount
        ).astype(BF)

    for base in (SIDE, NSIDE):
        shift(base, 48, left_bad)
        shift(base + 48, 48, right_bad)
    shift(FAR, 96, row_bad)
    shift(CORNER, 48, left_bad + row_bad)
    shift(CORNER + 48, 48, right_bad + row_bad)

    low = lane < 64
    zero = jnp.zeros((128, 128), BF)
    for i, base in enumerate((0, 384)):
        for h in range(PAIRS):
            part = kv[0:128, base + 128 * h : base + 128 * h + 128]
            bd[i, h, 0:128, :] = jnp.where(low, part, zero)
            bd[i, h, 128:256, :] = jnp.where(low, zero, part)
    acc[...] = jnp.zeros(acc.shape, F32)

    vec = lax.broadcasted_iota(jnp.int32, (1, 128), 1)
    lane_row = (vec // 16).astype(F32)
    lane_col = lax.rem(vec, 16).astype(F32)
    shift_open = math.log(25.0)

    slots = {NEAR: I_NEAR, SIDE: I_SIDE, NSIDE: I_NSIDE, FAR: I_FAR, CORNER: I_CORNER}

    def shifts(start, size):
        slot = slots.get(start, I_OWN)
        if start in (SIDE, NSIDE, CORNER):
            chosen = jnp.where(tile[0:size, 0:32] < 48, 1, 16) == lane[0:size, 0:32]
            table = jnp.concatenate([info[slot], info[slot + 1]], axis=0)
        else:
            chosen = lax.rem(tile[0:size, 0:16], 16) // 8 == lane[0:size, 0:16]
            table = info[slot]
        return dot(chosen.astype(F32).astype(BF), table).astype(BF)

    def attend(t, start, size):
        if t == 0:
            where_at = place[start : start + size, :] + shifts(start, size)
            at = dot(where_at, spread_ref[...])
            gap = jnp.maximum(
                jnp.abs(at[:, 0:128] - lane_row), jnp.abs(at[:, 128:256] - lane_col)
            )
            bias = jnp.where(gap <= 2.5, shift_open, 1e9)
            closed[start : start + size, :] = bias
        else:
            bias = closed[start : start + size, :]
        bias = jnp.concatenate([bias, bias], axis=1)
        for h in GROUPS[t][0]:
            one = qg[start : start + size, 256 * h : 256 * h + 128]
            two = qg[start : start + size, 256 * h + 128 : 256 * h + 256]
            score = dot(one, bd[0, h], ((1,), (1,)))
            dweight = dot(two, bd[1, h], ((1,), (1,)))
            e = jnp.exp(jnp.minimum(bias - score * 0.125, 88.0))
            sig = 1.0 / (1.0 + e)
            dscore = (dweight * (sig * (1.0 - sig))).astype(BF)
            acc[0, h] += dot(dscore, one, ((0,), (0,)))
            acc[1, h] += dot(sig.astype(BF), two, ((0,), (0,)))
            back = dot(dscore, bd[0, h]) * 0.125
            dqp[start : start + size, 128 * h : 128 * h + 128] = back.astype(BF)

    def gather(i, scale):
        parts = [jnp.where(low, acc[i, h, 0:128], acc[i, h, 128:256]) * scale for h in range(PAIRS)]
        return jnp.concatenate(parts, axis=1)

    def arrived(t, *names):
        for name in names:
            if t == 0:
                cps[name, 2].wait_recv()
            cps[name, t].wait_recv()

    attend(0, OWN, 128)
    attend(1, OWN, 128)
    for t, (_, lanes, part) in enumerate(GROUPS):
        arrived(t, "near")
        attend(t, NEAR, 96)
        near_rows = (rng(NEAR), part)
        cps["near", 3 + t] = send(
            dqp.at[near_rows], dqr.at[near_rows], S_NEAR + 3 + t, near
        )
        arrived(t, "right", "left")
        if t == 0:
            cps["fwd", 2] = send(
                info.at[pl.ds(I_SIDE, 2)], info.at[pl.ds(I_NSIDE, 2)], S_FWD + 2, near
            )
        cps["fwd", t] = send(
            qg.at[rng(SIDE), lanes], qg.at[rng(NSIDE), lanes], S_FWD + t, near
        )
        attend(t, SIDE, 96)
        arrived(t, "far")
        attend(t, FAR, 96)
        far_rows = (rng(FAR), part)
        cps["far", 3 + t] = send(dqp.at[far_rows], dqr.at[far_rows], S_FAR + 3 + t, far)
        arrived(t, "fwd")
        attend(t, NSIDE, 96)
        cps["fwd", 3 + t] = send(
            dqp.at[rng(NSIDE), part], dqn.at[rng(0), part], S_FWD + 3 + t, near
        )
        arrived(t, "cr", "cl")
        attend(t, CORNER, 96)
        one, two = (rng(CORNER, 48), part), (rng(CORNER + 48, 48), part)
        cps["cr", 3 + t] = send(dqp.at[one], dqr.at[one], S_CR + 3 + t, far_left)
        cps["cl", 3 + t] = send(dqp.at[two], dqr.at[two], S_CL + 3 + t, far_right)
        cps["fwd", 3 + t].wait_recv()
        side_sum[:, part] = (
            dqp[SIDE : SIDE + 96, part].astype(F32) + dqn[:, part].astype(F32)
        ).astype(BF)
        cps["right", 3 + t] = send(
            side_sum.at[rng(0, 48), part], dqr.at[rng(SIDE, 48), part], S_RIGHT + 3 + t, left
        )
        cps["left", 3 + t] = send(
            side_sum.at[rng(48, 48), part], dqr.at[rng(SIDE + 48, 48), part],
            S_LEFT + 3 + t, right,
        )

    dk = gather(0, 0.125).astype(BF)
    dv = (gather(1, 1.0) * key_open).astype(BF)
    dmine[1] = dk
    dmine[2] = dv
    cps["dkv"] = send(dmine.at[pl.ds(1, 2)], dother.at[pl.ds(1, 2)], S_DKV, near)
    cps["hx"].wait_recv()
    cps["dkv"].wait_recv()

    def partial(m, t):
        total = dot(hp[core, t], dmine[m], ((0,), (0,)))
        return total + dot(hx[t], dother[m], ((0,), (0,)))

    for m in (1, 2):
        w = partial(m, 1)
        for i in range(nx):
            piece = w[96 * i : 96 * i + 96]
            dw[i, :, 384 * m : 384 * m + 384] = piece
            xs_kv[m - 1, i] = piece.astype(BF)
        for v, d in x_peers:
            cps["xkv", m, d] = send(
                xs_kv.at[m - 1, v], xr_kv.at[m - 1, d - 1], S_X + 3 * m + d - 1, x_dev(v)
            )
    ihcg_ref[...] = (
        dot(dk, wk_ref[...], ((1,), (1,))) + dot(dv, wv_ref[...], ((1,), (1,)))
    ).astype(BF)
    leave(1, ihcg_ref, ihcg_out)
    dqa[...] = dqp[0:128, :].astype(F32)
    for t in range(2):
        cps["near", 3 + t].wait_recv()
    dqa[near_at, :] += dqr[NEAR : NEAR + 96, :].astype(F32)
    for name in ("far", "cr", "cl", "right", "left"):
        for t in range(2):
            cps[name, 3 + t].wait_recv()
    dqa[far_at, :] += dqr[FAR : FAR + 96, :].astype(F32)
    edges = dot(pack_ref[...], dqr[SIDE : SIDE + 96, :], ((0,), (0,)))
    edges = edges + dot(pack_ref[...], dqr[CORNER : CORNER + 96, :], ((0,), (0,)))
    dq = (dqa[...] + edges).astype(BF)
    dmine[0] = dq
    cps["dq"] = send(dmine.at[0], dother.at[0], S_DQ, near)
    heg_ref[...] = dot(dq, wq_ref[...], ((1,), (1,))).astype(BF)
    leave(0, heg_ref, heg_out)
    cps["dq"].wait_recv()
    w = partial(0, 0)
    for i in range(nx):
        piece = w[96 * i : 96 * i + 96]
        dw[i, :, 0:384] = piece
        xs_q[i] = piece.astype(BF)
    for v, d in x_peers:
        cps["xq", d] = send(xs_q.at[v], xr_q.at[d - 1], S_X + d - 1, x_dev(v))
    def to_y(dst, at, total):
        laid = dot(total.astype(BF), toy_ref[...]).astype(BF)
        for h in range(2):
            for l in range(4):
                dst[4 * h + l, :, 128 * at : 128 * at + 128] = laid[
                    48 * h : 48 * h + 48, 128 * l : 128 * l + 128
                ]

    for m in (1, 2):
        for _, d in x_peers:
            cps["xkv", m, d].wait_recv()
        total = dw[x, :, 384 * m : 384 * m + 384]
        for _, d in x_peers:
            total = total + xr_kv[m - 1, d - 1].astype(F32)
        to_y(ys_kv, m - 1, total)
    for v, d in y_peers:
        cps["ykv", d] = send(ys_kv.at[v], yr_kv.at[d - 1], S_YKV + d - 1, y_dev(v))
    for _, d in x_peers:
        cps["xq", d].wait_recv()
    total = dw[x, :, 0:384]
    for _, d in x_peers:
        total = total + xr_q[d - 1].astype(F32)
    to_y(ys_q, 0, total)
    for v, d in y_peers:
        cps["yq", d] = send(ys_q.at[v], yr_q.at[d - 1], S_YQ + d - 1, y_dev(v))
    total_kv = ys_kv[y].astype(F32)
    for _, d in y_peers:
        cps["ykv", d].wait_recv()
        total_kv = total_kv + yr_kv[d - 1].astype(F32)
    total_q = ys_q[y].astype(F32)
    for _, d in y_peers:
        cps["yq", d].wait_recv()
        total_q = total_q + yr_q[d - 1].astype(F32)
    total = jnp.concatenate([total_q, total_kv], axis=1)
    laid = dot(total.astype(BF), toz_ref[...]).astype(BF)
    for i in range(nz):
        zs[i] = laid[:, 128 * i : 128 * i + 128]
    for v, d in z_peers:
        cps["z", d] = send(zs.at[v], zr.at[d - 1], S_Z + d - 1, z_dev(v))
    total = zs[z].astype(F32)
    for _, d in z_peers:
        cps["z", d].wait_recv()
        total = total + zr[d - 1].astype(F32)
    total = total * (1.0 / math.sqrt(128.0 * rows * cols))
    turned = total.T
    for m in range(3):
        wg_ref[m] = turned[12 * m : 12 * m + 12, :]
    leave(2, wg_ref, wg_out)
    for cp in started:
        cp.wait_send()
    for cp in outs:
        cp.wait()


def write_out(a_in, b_in, c_in, a_out, b_out, c_out, a, b, c, sem):
    held = ((a_in, a, a_out), (b_in, b, b_out), (c_in, c, c_out))
    loads = [pltpu.make_async_copy(h[0], h[1], sem.at[0, i]) for i, h in enumerate(held)]
    stores = [pltpu.make_async_copy(h[1], h[2], sem.at[1, i]) for i, h in enumerate(held)]
    for cp in loads:
        cp.start()
    for load, store in zip(loads, stores):
        load.wait()
        store.start()
    for cp in stores:
        cp.wait()


def on_device(rows, cols, he, ihc, he_mask, ihc_mask, offsets, wq, wk, wv, grad_out):
    nx, nz = rows // 4, cols // 4
    consts = constants()
    args = (
        offsets,
        he.reshape(128, 768), ihc.reshape(128, 768),
        he_mask, ihc_mask,
        wq, wk, wv, grad_out.reshape(128, 384), *consts,
    )
    heg, ihcg, wg = pl.pallas_call(
        functools.partial(kernel, rows, cols),
        out_shape=(
            jax.ShapeDtypeStruct((128, 768), BF),
            jax.ShapeDtypeStruct((128, 768), BF),
            jax.ShapeDtypeStruct((3, 12, 48), F32),
        ),
        in_specs=[pl.BlockSpec(memory_space=pltpu.HBM)] * len(args),
        out_specs=[pl.BlockSpec(memory_space=pltpu.HBM)] * 3,
        scratch_shapes=[
            pltpu.VMEM((128, 768), BF),
            pltpu.VMEM((128, 768), BF),
            pltpu.VMEM((3, 12, 48), F32),
            pltpu.SemaphoreType.DMA((3,)),
        ]
        + [pltpu.VMEM(a.shape, a.dtype) for a in args]
        + [
            pltpu.SemaphoreType.DMA((len(args),)),
            pltpu.VMEM((ROWS, 768), BF),
            pltpu.VMEM((128, 768), BF),
            pltpu.VMEM((96, 768), BF),
            pltpu.VMEM((I_ALL, 16, 128), BF),
            pltpu.VMEM((ROWS, 128), BF),
            pltpu.VMEM((2, PAIRS, 256, 128), BF),
            pltpu.VMEM((2, PAIRS, 256, 128), F32),
            pltpu.VMEM((ROWS, 128), F32),
            pltpu.VMEM((ROWS, 384), BF),
            pltpu.VMEM((ROWS, 384), BF),
            pltpu.VMEM((96, 384), BF),
            pltpu.VMEM((96, 384), BF),
            pltpu.VMEM((128, 384), F32),
            pltpu.VMEM((2, 2, 128, 384), BF),
            pltpu.VMEM((2, 128, 384), BF),
            pltpu.VMEM((3, 128, 384), BF),
            pltpu.VMEM((3, 128, 384), BF),
            pltpu.VMEM((nx, 96, 1152), F32),
            pltpu.VMEM((nx, 96, 384), BF),
            pltpu.VMEM((nx - 1, 96, 384), BF),
            pltpu.VMEM((2, nx, 96, 384), BF),
            pltpu.VMEM((2, nx - 1, 96, 384), BF),
            pltpu.VMEM((8, 48, 128), BF),
            pltpu.VMEM((7, 48, 128), BF),
            pltpu.VMEM((8, 48, 256), BF),
            pltpu.VMEM((7, 48, 256), BF),
            pltpu.VMEM((nz, 48, 128), BF),
            pltpu.VMEM((nz - 1, 48, 128), BF),
            pltpu.SemaphoreType.DMA((S_ALL,)),
            pltpu.SemaphoreType.DMA((S_ALL,)),
        ],
        compiler_params=pltpu.CompilerParams(
            collective_id=0, has_side_effects=True, vmem_limit_bytes=56 << 20
        ),
    )(*args)
    parts = (heg, ihcg, wg)
    heg, ihcg, wg = pl.pallas_call(
        write_out,
        out_shape=tuple(jax.ShapeDtypeStruct(a.shape, a.dtype) for a in parts),
        in_specs=[pl.BlockSpec(memory_space=pl.ANY)] * 3,
        out_specs=[pl.BlockSpec(memory_space=pltpu.HBM)] * 3,
        scratch_shapes=[pltpu.VMEM(a.shape, a.dtype) for a in parts]
        + [pltpu.SemaphoreType.DMA((2, 3))],
        compiler_params=pltpu.CompilerParams(vmem_limit_bytes=60 << 20),
    )(*parts)
    return heg.reshape(8, 16, 768), ihcg.reshape(8, 16, 768), jnp.swapaxes(wg, 1, 2)


def solution(mesh):
    placed = (
        P("row", "col", None), P("row", "col", None), P("row", "col"), P("row", "col"),
        P("row", "col", None), P(), P(), P(), P("row", "col", None),
    )
    return jax.shard_map(
        functools.partial(on_device, mesh.shape["row"], mesh.shape["col"]),
        mesh=mesh,
        in_specs=placed,
        out_specs=(P("row", "col", None), P("row", "col", None), P(None, "row", "col")),
        check_vma=False,
    )
```
